32 devices in a mesh: ex: 16 (over z, y, x), hh: 2 (over core).
Axes of the slice: x: 2, y: 2, z: 4, core: 2. Of those that a mesh axis runs over, the one named last changes fastest.
Arguments:
- moe_input: bfloat16 [8192, 512], P('ex'), may hold values from -6 to 6
- out_grad: bfloat16 [8192, 512], P('ex'), may hold values from -6 to 6
- gate: float32 [8192], P('ex'), may hold values from 0.2 to 1
- route: int32 [8192, 1], P('ex'), may hold values from 0 to 15; in each aligned block of 512 rows (0 to 511, 512 to 1023, ...) at most 64 rows name the same one
- w_in: bfloat16 [16, 512, 2048], P('ex', None, 'hh'), may hold values from -0.25 to 0.25
- b_in: float32 [16, 2048], P('ex', 'hh'), may hold values from -3 to 3
- w_out: bfloat16 [16, 2048, 512], P('ex', 'hh'), may hold values from -0.125 to 0.125
- qkv: bfloat16 [3, 8192, 512], P(None, 'ex', 'hh'), may hold values from -8 to 8
Outputs:
- g_w_in: float32 [16, 512, 2048], P('ex', None, 'hh')
- g_b_in: float32 [16, 2048], P('ex', 'hh')
- g_w_out: float32 [16, 2048, 512], P('ex', 'hh')
- g_qkv: bfloat16 [3, 8192, 512], P(None, 'ex', 'hh')
The draws below stay inside these ranges and needn't reach their ends.
Inputs may be any that keep to these rules, and one draw needn't show every extreme that they name: `route`: in the rows of one device no expert is named more than 64 times, a bound that some block reaches.
All inputs are finite; a program needn't handle non-finite values.
Results may differ from the reference program's by a relative error of at most 0.014.
Values may be sent and summed in bfloat16 or wider, within the bound.
A program may use at most 128 MiB of HBM per device.

```python
import math
import jax
import jax.numpy as jnp
import numpy as np
from jax import lax

D = 512
HEADS = 16
FF = 2048
CELLS = 64
WIN_T = 8
SHIFT = 4
EXPERTS = 16
TOK_DEV = 512
TOKENS = 8192
CAP = 64
N_EX = 16


def draw_qkv(key, part):
    base = jnp.clip(jax.random.normal(key, (3, TOKENS, D), jnp.float32), -6.0, 6.0)
    return base.astype(jnp.bfloat16)


def levels(own_key, extent, shards, smallest, largest):
    gain = 1.0
    for dim, parts in shards:
        heights = jax.random.uniform(jax.random.fold_in(jax.random.fold_in(own_key, 6), dim), (parts,), jnp.float32, smallest / len(shards), largest / len(shards))
        gain = gain * jnp.repeat(jnp.exp(heights), extent[dim] // parts).reshape((-1,) + (1,) * (len(extent) - 1 - dim))
    return gain


def shared_out(stream_key, own, number, rows, count, top, reach, skew):
    sequence = jax.random.permutation(stream_key, count)
    crowded, common = portions_of(count, rows * top, reach, skew, True), portions_of(count, rows * top, reach, skew, False)
    places = jnp.arange(count)

    def named(lengths, offset_by):
        used = int((lengths > 0).sum())
        fixed = max(1, used // 4)
        passed = fixed + (places - fixed + offset_by * (used - fixed)) % max(1, count - fixed)
        return jnp.zeros((count,), jnp.int32).at[sequence[jnp.where(places < fixed, places, passed)]].set(jnp.asarray(lengths, jnp.int32))

    lengths = jnp.where(number % 4 == 0, named(crowded, number // 4), named(common, number - number // 4 - 1))
    mixed = jax.random.permutation(jax.random.fold_in(own, 3), count)
    donor, sink = mixed[0:count // 2 * 2:2], mixed[1:count // 2 * 2:2]
    slack = jnp.minimum(lengths[donor] - 1, reach - lengths[sink]) // 2
    slack = jnp.where((donor == sequence[0]) | (sink == sequence[0]) | (lengths[sink] == 0), 0, jnp.maximum(slack, 0))
    passed = jax.random.randint(jax.random.fold_in(own, 4), (count // 2,), 0, 1 << 20) % (slack + 1)
    lengths = lengths.at[donor].add(-passed).at[sink].add(passed)
    items = jnp.searchsorted(jnp.cumsum(lengths), jnp.arange(rows * top), side="right").astype(jnp.int32)
    table = items.reshape(top, rows).T
    table = table[jax.random.permutation(jax.random.fold_in(own, 1), rows)]
    offset_by = jax.random.randint(jax.random.fold_in(own, 2), (rows, 1), 0, top)
    return jnp.take_along_axis(table, (jnp.arange(top)[None, :] + offset_by) % top, axis=1)


def portions_of(count, total, bound, skew, full):
    weights = [(1 << 20) // math.isqrt(standing ** skew) + 1 for standing in range(1, count + 1)]
    largest = bound if full else min(bound, max(-(-total // count), total * weights[0] // sum(weights)))
    least = 1 if total - largest >= count - 1 else 0
    holding, spare = [largest] + [least] * (count - 1), total - largest - least * (count - 1)
    while spare > 0:
        movable = [i for i in range(1, count) if holding[i] < largest] or [i for i in range(1, count) if holding[i] < bound]
        pool, budget = sum([weights[i] for i in movable]), spare
        for i in movable:
            extra = min(bound - holding[i], max(1, budget * weights[i] // pool), spare)
            holding[i] = holding[i] + extra
            spare = spare - extra
    return np.array(holding)


def gaussian(own_key, dims, width, reach, pieces=(), held_as=jnp.bfloat16):
    factor_of = levels(own_key, dims, pieces, -0.22, 0.18) if pieces else 1.0
    entries = jax.random.normal(own_key, dims, jnp.float32) * width * factor_of
    return jnp.minimum(jnp.maximum(entries, -reach), reach).astype(held_as)


def setup_inputs(seed: int = 0) -> dict:
    key_of = jax.random.split(jax.random.key(seed), 9)
    moe_input = gaussian(key_of[0], (TOKENS, D), 1.0, 6.0, ((0, 16),))
    out_grad = gaussian(key_of[1], (TOKENS, D), 1.0, 6.0, ((0, 16),))
    gate = jnp.clip(jnp.exp(math.log(1.0) - 1.609438 * jax.random.uniform(key_of[2], (TOKENS,), jnp.float32) ** levels(key_of[2], (TOKENS,), ((0, 16),), -0.2, 0.2)), 0.2, 1.0)
    route_keys = jax.random.split(jax.random.fold_in(key_of[3], 1), TOKENS // TOK_DEV)
    route_turns = jax.random.permutation(jax.random.fold_in(key_of[3], 3), TOKENS // TOK_DEV)
    route = jax.vmap(lambda own, number: shared_out(jax.random.fold_in(key_of[3], 2), own, number, TOK_DEV, EXPERTS, 1, CAP, 2))(route_keys, route_turns).reshape((TOKENS, 1))
    w_in = gaussian(key_of[4], (EXPERTS, D, FF), D ** -0.5, 0.25, ((0, 16), (2, 2)))
    b_in = gaussian(key_of[5], (EXPERTS, FF), 0.5, 3.0, ((0, 16), (1, 2)), jnp.float32)
    w_out = gaussian(key_of[6], (EXPERTS, FF, D), FF ** -0.5, 0.125, ((0, 16), (1, 2)))
    qkv = draw_qkv(jax.random.fold_in(key_of[8], 71), 0)
    return dict(moe_input=moe_input, out_grad=out_grad, gate=gate, route=route, w_in=w_in, b_in=b_in, w_out=w_out, qkv=qkv)


def gelu_parts(act):
    cdf = 0.5 * (1.0 + lax.erf(act * 0.7071067811865476))
    dens = jnp.exp(-0.5 * act * act) * 0.3989422804014327
    return act * cdf, cdf + act * dens


def expert_terms(inputs, scaled, w_first, bias, w_second):
    act = jnp.dot(inputs, w_first, preferred_element_type=jnp.float32) + bias
    value, slope = gelu_parts(act)
    hidden = value.astype(jnp.bfloat16)
    d_hidden = jnp.einsum("sd,fd->sf", scaled.astype(jnp.float32), w_second.astype(jnp.float32))
    d_pre = d_hidden * slope
    d_act = d_pre.astype(jnp.bfloat16)
    d_inputs = jnp.einsum("sf,df->sd", d_act.astype(jnp.float32), w_first.astype(jnp.float32))
    g_first = jnp.einsum("sd,sf->df", inputs.astype(jnp.float32), d_act.astype(jnp.float32))
    g_bias = jnp.sum(d_pre, axis=0)
    g_second = jnp.einsum("sf,sd->fd", hidden.astype(jnp.float32), scaled.astype(jnp.float32))
    return d_inputs.astype(jnp.bfloat16), g_first, g_bias, g_second


def window_grads(queries, keys, values, d_out, allowed, heads):
    rows, cols = queries.shape
    head_dim = cols // heads
    scale = head_dim ** -0.5
    qh = queries.reshape(rows, heads, head_dim).astype(jnp.float32)
    kh = keys.reshape(rows, heads, head_dim).astype(jnp.float32)
    vh = values.reshape(rows, heads, head_dim).astype(jnp.float32)
    oh = d_out.reshape(rows, heads, head_dim).astype(jnp.float32)
    scores = jnp.einsum("rhc,shc->hrs", qh, kh) * scale
    scores = jnp.where(allowed[None], scores, -1e30)
    peak = jnp.max(scores, axis=-1, keepdims=True)
    expo = jnp.exp(scores - peak)
    probs = expo / jnp.sum(expo, axis=-1, keepdims=True)
    probs_b = probs.astype(jnp.bfloat16)
    d_probs = jnp.einsum("rhc,shc->hrs", oh, vh)
    delta = jnp.sum(probs * d_probs, axis=-1, keepdims=True)
    d_scores = (probs * (d_probs - delta)).astype(jnp.bfloat16).astype(jnp.float32)
    d_q = (jnp.einsum("hrs,shc->rhc", d_scores, kh) * scale).astype(jnp.bfloat16)
    d_k = (jnp.einsum("hrs,rhc->shc", d_scores, qh) * scale).astype(jnp.bfloat16)
    d_v = jnp.einsum("hrs,rhc->shc", probs_b.astype(jnp.float32), oh).astype(jnp.bfloat16)
    return jnp.stack([d_q, d_k, d_v]).reshape(3, rows, cols)


def reference(moe_input, out_grad, gate, route, w_in, b_in, w_out, qkv):
    choose = route[:, 0]
    onehot = (choose[:, None] == jnp.arange(EXPERTS, dtype=jnp.int32)[None, :]).astype(jnp.int32)
    blocked = onehot.reshape(N_EX, TOK_DEV, EXPERTS)
    slots = (jnp.sum(jnp.cumsum(blocked, axis=1) * blocked, axis=2) - 1).reshape(TOKENS)
    source = jnp.arange(TOKENS, dtype=jnp.int32) // TOK_DEV
    dest = (choose * (N_EX * CAP) + source * CAP + slots).astype(jnp.int32)
    scaled = (gate[:, None] * out_grad.astype(jnp.float32)).astype(jnp.bfloat16)
    total = EXPERTS * N_EX * CAP
    buf_x = jnp.zeros((total, D), jnp.bfloat16).at[dest].set(moe_input).reshape(EXPERTS, N_EX * CAP, D)
    buf_s = jnp.zeros((total, D), jnp.bfloat16).at[dest].set(scaled).reshape(EXPERTS, N_EX * CAP, D)

    def per_expert(items):
        return expert_terms(items[0], items[1], items[2], items[3], items[4])

    d_rows, g_w_in, g_b_in, g_w_out = lax.map(per_expert, (buf_x, buf_s, w_in, b_in, w_out))
    d_moe = d_rows.reshape(total, D)[dest]
    d_heads = (out_grad.astype(jnp.float32) + d_moe.astype(jnp.float32)).astype(jnp.bfloat16)

    lead = SHIFT
    wrows = WIN_T * CELLS
    nwin = TOKENS // wrows
    rolled = jnp.roll(qkv, lead * CELLS, axis=1)
    cot = jnp.roll(d_heads, lead * CELLS, axis=0)
    wins = rolled.reshape(3, nwin, wrows, D).transpose(1, 0, 2, 3)
    cots = cot.reshape(nwin, wrows, D)
    rows = jnp.arange(wrows, dtype=jnp.int32)

    def per_window(items):
        index, block, d_out = items
        wrapped = (rows < lead * CELLS) & (index == 0)
        allowed = wrapped[:, None] == wrapped[None, :]
        return window_grads(block[0], block[1], block[2], d_out, allowed, HEADS)

    grads = lax.map(per_window, (jnp.arange(nwin, dtype=jnp.int32), wins, cots))
    grads = grads.transpose(1, 0, 2, 3).reshape(3, TOKENS, D)
    g_qkv = jnp.roll(grads, -lead * CELLS, axis=1)
    return (g_w_in, g_b_in, g_w_out, g_qkv)
```

```python
import functools
import math

import jax
import jax.numpy as jnp
from jax import lax
from jax.experimental import pallas as pl
from jax.experimental.pallas import tpu as pltpu
from jax.sharding import PartitionSpec as P

HEADS = 16
CELLS = 64
WIN_T = 8
SHIFT = 4


def passed_along(block, axis, distance):
    devices = range(lax.axis_size(axis))
    route = [((i - distance) % len(devices), i) for i in devices]
    return lax.ppermute(block, axis, route)


def gelu_parts(act):
    cdf = 0.5 * (1.0 + lax.erf(act * 0.7071067811865476))
    dens = jnp.exp(-0.5 * act * act) * 0.3989422804014327
    return (act * cdf, cdf + act * dens)


def expert_terms(inputs, scaled, w_first, bias, w_second):
    act = jnp.dot(inputs, w_first, preferred_element_type=jnp.float32) + bias
    value, slope = gelu_parts(act)
    hidden = value.astype(jnp.bfloat16)
    d_hidden = jnp.einsum("sd,fd->sf", scaled, w_second, preferred_element_type=jnp.float32)
    d_pre = d_hidden * slope
    d_act = d_pre.astype(jnp.bfloat16)
    d_inputs = jnp.einsum("sf,df->sd", d_act, w_first, preferred_element_type=jnp.float32)
    g_first = jnp.einsum("sd,sf->df", inputs, d_act, preferred_element_type=jnp.float32)
    g_bias = jnp.sum(d_pre, axis=0)
    g_second = jnp.einsum("sf,sd->fd", hidden, scaled, preferred_element_type=jnp.float32)
    return (d_inputs, g_first, g_bias, g_second)


def window_kernel(heads, bias_ref, edge_ref, own_ref, cot_edge_ref, cot_ref, back_ref, mine_ref,
                  q_t, k_t, cot_t, dq_t, dk_sum, dv_sum):
    lead = edge_ref.shape[1]
    rows, cols = q_t.shape[1], q_t.shape[0]
    head_dim = cols // heads
    scale = head_dim ** (-0.5)
    factor = scale * math.log2(math.e)
    queries = jnp.concatenate([edge_ref[0], own_ref[0, : rows - lead]], axis=0)
    keys = jnp.concatenate([edge_ref[1], own_ref[1, : rows - lead]], axis=0)
    values = jnp.concatenate([edge_ref[2], own_ref[2, : rows - lead]], axis=0)
    cot = jnp.concatenate([cot_edge_ref[...], cot_ref[: rows - lead]], axis=0)
    q_t[...] = queries.T
    k_t[...] = keys.T
    cot_t[...] = cot.T
    column = lax.broadcasted_iota(jnp.int32, (1, cols), 1)
    bias = bias_ref[0]
    for head in range(heads):
        own = (column // head_dim == head).astype(jnp.float32).astype(jnp.bfloat16)
        keys_h, values_h, queries_h, cot_h = keys * own, values * own, queries * own, cot * own
        d_k = d_v = None
        for part in range(2):
            span = slice(0, lead) if part == 0 else slice(lead, rows)
            scores = jnp.dot(keys_h, q_t[:, span], preferred_element_type=jnp.float32)
            low, high = scores[:lead], scores[lead:]
            if part == 0:
                high = high + bias
            else:
                low = low + bias
            scores = jnp.concatenate([low, high], axis=0)
            peak = jnp.max(scores, axis=0, keepdims=True)
            expo = jnp.exp2((scores - peak) * factor)
            probs = expo * (1.0 / jnp.sum(expo, axis=0, keepdims=True))
            d_probs = jnp.dot(values_h, cot_t[:, span], preferred_element_type=jnp.float32)
            delta = jnp.sum(probs * d_probs, axis=0, keepdims=True)
            d_scores = (probs * (d_probs - delta)).astype(jnp.bfloat16)
            probs_b = probs.astype(jnp.bfloat16)
            mine = slice(head * head_dim, (head + 1) * head_dim)
            dq_t[mine, span] = jnp.dot(k_t[mine, :], d_scores, preferred_element_type=jnp.float32) * scale
            more_k = jnp.dot(d_scores, queries_h[span], preferred_element_type=jnp.float32)
            more_v = jnp.dot(probs_b, cot_h[span], preferred_element_type=jnp.float32)
            d_k = more_k if d_k is None else d_k + more_k
            d_v = more_v if d_v is None else d_v + more_v
        if head == 0:
            dk_sum[...] = d_k
            dv_sum[...] = d_v
        else:
            dk_sum[...] += d_k
            dv_sum[...] += d_v
    d_q = dq_t[...].T.astype(jnp.bfloat16)
    d_k = (dk_sum[...] * scale).astype(jnp.bfloat16)
    d_v = dv_sum[...].astype(jnp.bfloat16)
    for place, grad in enumerate((d_q, d_k, d_v)):
        back_ref[place] = grad[:lead]
        mine_ref[place] = grad[lead:]


def window_grads(bias, edge, own, cot_edge, cot, heads):
    lead = edge.shape[1]
    rows, cols = cot.shape
    vmem = pl.BlockSpec(memory_space=pltpu.VMEM)
    return pl.pallas_call(
        functools.partial(window_kernel, heads),
        out_shape=(
            jax.ShapeDtypeStruct((3, lead, cols), jnp.bfloat16),
            jax.ShapeDtypeStruct((3, rows - lead, cols), jnp.bfloat16),
        ),
        in_specs=[pl.BlockSpec(memory_space=pltpu.SMEM)] + [vmem] * 4,
        out_specs=(vmem, vmem),
        scratch_shapes=[
            pltpu.VMEM((cols, rows), jnp.bfloat16),
            pltpu.VMEM((cols, rows), jnp.bfloat16),
            pltpu.VMEM((cols, rows), jnp.bfloat16),
            pltpu.VMEM((cols, rows), jnp.float32),
            pltpu.VMEM((rows, cols), jnp.float32),
            pltpu.VMEM((rows, cols), jnp.float32),
        ],
        compiler_params=pltpu.CompilerParams(vmem_limit_bytes=48 * 1024 * 1024),
        cost_estimate=pl.CostEstimate(
            flops=10 * rows * rows * cols, bytes_accessed=14 * rows * cols, transcendentals=heads * rows * rows
        ),
        name="window_grads",
    )(bias, edge, own, cot_edge, cot)


def local(moe_input, out_grad, gate, route, w_in, b_in, w_out, qkv):
    tok_rows, width = moe_input.shape
    experts = lax.axis_size("ex")
    capacity = max(2, 2 * tok_rows // experts)
    half = width // lax.axis_size("hh")
    member = lax.axis_index("hh")
    heads_here = HEADS // lax.axis_size("hh")
    lead = SHIFT * CELLS
    start = WIN_T * CELLS - lead
    qkv_edge = passed_along(qkv[:, start:], "ex", 1)
    choose = route[:, 0]
    onehot = (choose[:, None] == jnp.arange(experts, dtype=jnp.int32)[None, :]).astype(jnp.bfloat16)
    earlier = (jnp.arange(tok_rows)[:, None] > jnp.arange(tok_rows)[None, :]).astype(jnp.bfloat16)
    before = jnp.dot(earlier, onehot, preferred_element_type=jnp.float32)
    slots = jnp.sum(before * onehot.astype(jnp.float32), axis=1).astype(jnp.int32)
    dest = choose * capacity + slots
    place = (dest[None, :] == jnp.arange(experts * capacity, dtype=jnp.int32)[:, None]).astype(jnp.bfloat16)
    own_x = lax.dynamic_slice_in_dim(moe_input, member * half, half, 1)
    own_grad = lax.dynamic_slice_in_dim(out_grad, member * half, half, 1)
    own_s = (gate[:, None] * own_grad.astype(jnp.float32)).astype(jnp.bfloat16)
    tokens = jnp.concatenate([own_x, own_s], axis=1)
    send = jnp.dot(place, tokens, preferred_element_type=jnp.float32).astype(jnp.bfloat16)
    send = send.reshape(experts, capacity, 2 * half)
    got = lax.all_to_all(send, "ex", split_axis=0, concat_axis=0, tiled=True)
    got = got.reshape(experts * capacity, 2 * half)
    other = passed_along(got, "hh", 1)
    first, second = jnp.where(member == 0, got, other), jnp.where(member == 0, other, got)
    got_x = jnp.concatenate([first[:, :half], second[:, :half]], axis=1)
    got_s = jnp.concatenate([first[:, half:], second[:, half:]], axis=1)
    d_inputs, g_first, g_bias, g_second = expert_terms(got_x, got_s, w_in[0], b_in[0], w_out[0])
    kept = lax.dynamic_slice_in_dim(d_inputs, member * half, half, 1)
    given = lax.dynamic_slice_in_dim(d_inputs, (1 - member) * half, half, 1).astype(jnp.bfloat16)
    d_rows = (kept + passed_along(given, "hh", 1).astype(jnp.float32)).astype(jnp.bfloat16)
    returned = lax.all_to_all(
        d_rows.reshape(experts, capacity, half), "ex", split_axis=0, concat_axis=0, tiled=True
    ).reshape(experts * capacity, half)
    d_moe = lax.dot_general(place, returned, (((0,), (0,)), ((), ())), preferred_element_type=jnp.float32)
    d_heads = (own_grad.astype(jnp.float32) + d_moe).astype(jnp.bfloat16)
    cot_edge = passed_along(d_heads[start:], "ex", 1)
    bias = jnp.where(lax.axis_index("ex") == 0, -1e30, 0.0).astype(jnp.float32).reshape(1)
    back, mine = window_grads(bias, qkv_edge, qkv, cot_edge, d_heads, heads_here)
    g_qkv = jnp.concatenate([mine, passed_along(back, "ex", -1)], axis=1)
    return (g_first[None], g_bias[None], g_second[None], g_qkv)


def solution(mesh):
    in_specs = (
        P("ex", None),
        P("ex", None),
        P("ex"),
        P("ex", None),
        P("ex", None, "hh"),
        P("ex", "hh"),
        P("ex", "hh", None),
        P(None, "ex", "hh"),
    )
    out_specs = (P("ex", None, "hh"), P("ex", "hh"), P("ex", "hh", None), P(None, "ex", "hh"))
    return jax.shard_map(local, mesh=mesh, in_specs=in_specs, out_specs=out_specs, check_vma=False)
```

```python
import functools
import math

import jax
import jax.numpy as jnp
from jax import lax
from jax.experimental import pallas as pl
from jax.experimental.pallas import tpu as pltpu
from jax.sharding import PartitionSpec as P

HEADS = 16
CELLS = 64
WIN_T = 8
SHIFT = 4


def passed_along(block, axis, distance):
    devices = range(lax.axis_size(axis))
    route = [((i - distance) % len(devices), i) for i in devices]
    return lax.ppermute(block, axis, route)


def gelu_parts(act):
    cdf = 0.5 * (1.0 + lax.erf(act * 0.7071067811865476))
    dens = jnp.exp(-0.5 * act * act) * 0.3989422804014327
    return (act * cdf, cdf + act * dens)


def expert_terms(inputs, scaled, w_first, bias, w_second):
    act = jnp.dot(inputs, w_first, preferred_element_type=jnp.float32) + bias
    value, slope = gelu_parts(act)
    hidden = value.astype(jnp.bfloat16)
    d_hidden = jnp.einsum("sd,fd->sf", scaled, w_second, preferred_element_type=jnp.float32)
    d_pre = d_hidden * slope
    d_act = d_pre.astype(jnp.bfloat16)
    d_inputs = jnp.einsum("sf,df->sd", d_act, w_first, preferred_element_type=jnp.float32)
    g_first = jnp.einsum("sd,sf->df", inputs, d_act, preferred_element_type=jnp.float32)
    g_bias = jnp.sum(d_pre, axis=0)
    g_second = jnp.einsum("sf,sd->fd", hidden, scaled, preferred_element_type=jnp.float32)
    return (d_inputs, g_first, g_bias, g_second)


def window_kernel(heads, bias_ref, edge_ref, own_ref, cot_edge_ref, cot_ref, back_ref, mine_ref,
                  q_t, k_t, cot_t, dq_t, dk_sum, dv_sum):
    lead = edge_ref.shape[1]
    rows, cols = q_t.shape[1], q_t.shape[0]
    head_dim = cols // heads
    scale = head_dim ** (-0.5)
    factor = scale * math.log2(math.e)
    queries = jnp.concatenate([edge_ref[0], own_ref[0, : rows - lead]], axis=0)
    keys = jnp.concatenate([edge_ref[1], own_ref[1, : rows - lead]], axis=0)
    values = jnp.concatenate([edge_ref[2], own_ref[2, : rows - lead]], axis=0)
    cot = jnp.concatenate([cot_edge_ref[...], cot_ref[: rows - lead]], axis=0)
    q_t[...] = queries.T
    k_t[...] = keys.T
    cot_t[...] = cot.T
    column = lax.broadcasted_iota(jnp.int32, (1, cols), 1)
    bias = bias_ref[0]
    for head in range(heads):
        own = (column // head_dim == head).astype(jnp.float32).astype(jnp.bfloat16)
        keys_h, values_h, queries_h, cot_h = keys * own, values * own, queries * own, cot * own
        d_k = d_v = None
        for part in range(2):
            span = slice(0, lead) if part == 0 else slice(lead, rows)
            scores = jnp.dot(keys_h, q_t[:, span], preferred_element_type=jnp.float32)
            low, high = scores[:lead], scores[lead:]
            if part == 0:
                high = high + bias
            else:
                low = low + bias
            scores = jnp.concatenate([low, high], axis=0)
            peak = jnp.max(scores, axis=0, keepdims=True)
            expo = jnp.exp2((scores - peak) * factor)
            probs = expo * (1.0 / jnp.sum(expo, axis=0, keepdims=True))
            d_probs = jnp.dot(values_h, cot_t[:, span], preferred_element_type=jnp.float32)
            delta = jnp.sum(probs * d_probs, axis=0, keepdims=True)
            d_scores = (probs * (d_probs - delta)).astype(jnp.bfloat16)
            probs_b = probs.astype(jnp.bfloat16)
            mine = slice(head * head_dim, (head + 1) * head_dim)
            dq_t[mine, span] = jnp.dot(k_t[mine, :], d_scores, preferred_element_type=jnp.float32) * scale
            more_k = jnp.dot(d_scores, queries_h[span], preferred_element_type=jnp.float32)
            more_v = jnp.dot(probs_b, cot_h[span], preferred_element_type=jnp.float32)
            d_k = more_k if d_k is None else d_k + more_k
            d_v = more_v if d_v is None else d_v + more_v
        if head == 0:
            dk_sum[...] = d_k
            dv_sum[...] = d_v
        else:
            dk_sum[...] += d_k
            dv_sum[...] += d_v
    d_q = dq_t[...].T.astype(jnp.bfloat16)
    d_k = (dk_sum[...] * scale).astype(jnp.bfloat16)
    d_v = dv_sum[...].astype(jnp.bfloat16)
    for place, grad in enumerate((d_q, d_k, d_v)):
        back_ref[place] = grad[:lead]
        mine_ref[place] = grad[lead:]


def window_grads(bias, edge, own, cot_edge, cot, heads):
    lead = edge.shape[1]
    rows, cols = cot.shape
    vmem = pl.BlockSpec(memory_space=pltpu.VMEM)
    return pl.pallas_call(
        functools.partial(window_kernel, heads),
        out_shape=(
            jax.ShapeDtypeStruct((3, lead, cols), jnp.bfloat16),
            jax.ShapeDtypeStruct((3, rows - lead, cols), jnp.bfloat16),
        ),
        in_specs=[pl.BlockSpec(memory_space=pltpu.SMEM)] + [vmem] * 4,
        out_specs=(vmem, vmem),
        scratch_shapes=[
            pltpu.VMEM((cols, rows), jnp.bfloat16),
            pltpu.VMEM((cols, rows), jnp.bfloat16),
            pltpu.VMEM((cols, rows), jnp.bfloat16),
            pltpu.VMEM((cols, rows), jnp.float32),
            pltpu.VMEM((rows, cols), jnp.float32),
            pltpu.VMEM((rows, cols), jnp.float32),
        ],
        compiler_params=pltpu.CompilerParams(vmem_limit_bytes=48 * 1024 * 1024),
        cost_estimate=pl.CostEstimate(
            flops=10 * rows * rows * cols, bytes_accessed=14 * rows * cols, transcendentals=heads * rows * rows
        ),
        name="window_grads",
    )(bias, edge, own, cot_edge, cot)

MESH = pl.DeviceIdType.MESH


def exchange_kernel(n, group, send_ref, qkv_ref, w_in_ref, b_ref, w_out_ref, place_t_ref, grad_ref,
                    got_ref, dact_ref, hidden_ref, gb_ref, edge_ref, cot_edge_ref, heads_ref,
                    w_in_t, w_out_t, part_out, part_in, ret_out, ret_in,
                    send_sem, recv_sem, on_send, on_recv, part_send, part_recv, ret_send, ret_recv,
                    edge_sem, cot_sem, own_sem):
    me, core = lax.axis_index("ex"), lax.axis_index("hh")
    after, sibling = lax.rem(me + 1, n), 1 - core
    capacity, half = ret_in.shape[1], ret_in.shape[2]
    rows = group * capacity
    lead = edge_ref.shape[1]
    start = qkv_ref.shape[1] - lead
    hidden_units = w_in_ref.shape[1]
    bits = n.bit_length() - 1

    def partner(k):
        total = 0
        for b in range(bits):
            bit = lax.rem(lax.div(me, 1 << b), 2)
            total = total + ((1 - bit) if (k >> b) & 1 else bit) * (1 << b)
        return total

    partners = [partner(k) for k in range(n)]
    barrier = pltpu.get_barrier_semaphore()
    for k in range(1, n):
        pl.semaphore_signal(barrier, inc=1, device_id=(partners[k], core), device_id_type=MESH)
    pl.semaphore_signal(barrier, inc=1, device_id=(me, sibling), device_id_type=MESH)
    pl.semaphore_wait(barrier, n)

    def remote(src, dst, send, recv, device):
        return pltpu.make_async_remote_copy(
            src_ref=src, dst_ref=dst, send_sem=send, recv_sem=recv, device_id=device, device_id_type=MESH
        )

    out = {
        k: remote(send_ref.at[partners[k]], got_ref.at[core, me], send_sem.at[k], recv_sem.at[k],
                  (partners[k], core))
        for k in range(1, n)
    }
    passed = {
        k: remote(got_ref.at[core, partners[k]], got_ref.at[core, partners[k]], on_send.at[k], on_recv.at[k],
                  (me, sibling))
        for k in range(n)
    }
    far = list(range(n // 2, n))
    near = list(range(1, n // 2))
    order = []
    while far or near:
        order += far[:2] + near[:1]
        far, near = far[2:], near[1:]
    for k in order:
        out[k].start()
    own = pltpu.make_async_copy(send_ref.at[me], got_ref.at[core, me], own_sem.at[0])
    own.start()
    edge = remote(qkv_ref.at[:, pl.ds(start, lead)], edge_ref, edge_sem.at[0], edge_sem.at[1], (after, core))
    edge.start()
    w_in_t[...] = w_in_ref[...].T
    w_out_t[...] = w_out_ref[...].T

    back = {}
    parts = []
    step = hidden_units // 4
    bias_sums = [0.0] * 4
    for g in range(n // group):
        ks = range(g * group, (g + 1) * group)
        for k in ks:
            if k == 0:
                own.wait()
            else:
                out[k].wait_recv()
            passed[k].start()
        for k in ks:
            passed[k].wait_recv()
        base = lax.div(partners[g * group], group) * group
        low = got_ref[0, pl.ds(base, group)].reshape(rows, 2 * half)
        high = got_ref[1, pl.ds(base, group)].reshape(rows, 2 * half)
        x = jnp.concatenate([low[:, :half], high[:, :half]], axis=1)
        s = jnp.concatenate([low[:, half:], high[:, half:]], axis=1)
        span = pl.ds(pl.multiple_of(base * capacity, rows), rows)
        d_rows = None
        for c in range(4):
            cols = slice(c * step, (c + 1) * step)
            act = jnp.dot(x, w_in_ref[:, cols], preferred_element_type=jnp.float32) + b_ref[:, cols]
            value, slope = gelu_parts(act)
            hidden_ref[span, cols] = value.astype(jnp.bfloat16)
            d_pre = jnp.dot(s, w_out_t[:, cols], preferred_element_type=jnp.float32) * slope
            d_act = d_pre.astype(jnp.bfloat16)
            dact_ref[span, cols] = d_act
            bias_sums[c] = bias_sums[c] + jnp.sum(d_pre, axis=0, keepdims=True)
            more = jnp.dot(d_act, w_in_t[cols, :], preferred_element_type=jnp.float32)
            d_rows = more if d_rows is None else d_rows + more
        kept = jnp.where(core == 0, d_rows[:, :half], d_rows[:, half:])
        given = jnp.where(core == 0, d_rows[:, half:], d_rows[:, :half])
        part_out[g] = given.astype(jnp.bfloat16)
        swap = remote(part_out.at[g], part_in.at[g], part_send.at[g], part_recv.at[g], (me, sibling))
        swap.start()
        parts.append(swap)
        swap.wait_recv()
        total = (kept + part_in[g].astype(jnp.float32)).astype(jnp.bfloat16)
        ret_out[pl.ds(base, group)] = total.reshape(group, capacity, half)
        for k in reversed(ks):
            if k == 0:
                back[k] = pltpu.make_async_copy(ret_out.at[me], ret_in.at[me], own_sem.at[1])
            else:
                back[k] = remote(ret_out.at[partners[k]], ret_in.at[me], ret_send.at[k], ret_recv.at[k],
                                 (partners[k], core))
            back[k].start()
    for c in range(4):
        gb_ref[:, c * step : (c + 1) * step] = bias_sums[c]

    total = grad_ref[...].astype(jnp.float32)
    for g in range(n // group):
        for k in range(g * group, (g + 1) * group):
            if k == 0:
                back[k].wait()
            else:
                back[k].wait_recv()
        base = lax.div(partners[g * group], group) * group
        span = pl.ds(pl.multiple_of(base * capacity, rows), rows)
        total = total + jnp.dot(
            place_t_ref[:, span], ret_in[pl.ds(base, group)].reshape(rows, half),
            preferred_element_type=jnp.float32,
        )
    heads_ref[...] = total.astype(jnp.bfloat16)
    cot = remote(heads_ref.at[pl.ds(start, lead)], cot_edge_ref, cot_sem.at[0], cot_sem.at[1], (after, core))
    cot.start()
    for k in range(n):
        passed[k].wait_send()
        if k > 0:
            out[k].wait_send()
            back[k].wait_send()
    for swap in parts:
        swap.wait_send()
    edge.wait()
    cot.wait()


def exchange(send, qkv, w_in, b_in, w_out, place_t, own_grad, lead):
    n, capacity, columns = send.shape
    half = columns // 2
    width, hidden_units = w_in.shape
    group = 4
    vmem = pl.BlockSpec(memory_space=pltpu.VMEM)
    bf16, f32 = jnp.bfloat16, jnp.float32
    dma = pltpu.SemaphoreType.DMA
    shape = jax.ShapeDtypeStruct
    return pl.pallas_call(
        functools.partial(exchange_kernel, n, group),
        out_shape=(
            shape((2, n, capacity, columns), bf16),
            shape((n * capacity, hidden_units), bf16),
            shape((n * capacity, hidden_units), bf16),
            shape((1, hidden_units), f32),
            shape((3, lead, half), bf16),
            shape((lead, half), bf16),
            shape(own_grad.shape, bf16),
        ),
        in_specs=[vmem] * 7,
        out_specs=[vmem] * 7,
        scratch_shapes=[
            pltpu.VMEM((hidden_units, width), bf16),
            pltpu.VMEM((width, hidden_units), bf16),
            pltpu.VMEM((n // group, group * capacity, half), bf16),
            pltpu.VMEM((n // group, group * capacity, half), bf16),
            pltpu.VMEM((n, capacity, half), bf16),
            pltpu.VMEM((n, capacity, half), bf16),
            dma((n,)), dma((n,)), dma((n,)), dma((n,)),
            dma((n // group,)), dma((n // group,)),
            dma((n,)), dma((n,)),
            dma((2,)), dma((2,)), dma((2,)),
        ],
        compiler_params=pltpu.CompilerParams(
            collective_id=0, has_side_effects=True, vmem_limit_bytes=48 * 1024 * 1024
        ),
        cost_estimate=pl.CostEstimate(
            flops=6 * n * capacity * width * hidden_units, bytes_accessed=16 * 1024 * 1024,
            transcendentals=2 * n * capacity * hidden_units,
        ),
        name="exchange",
    )(send, qkv, w_in, b_in, w_out, place_t, own_grad)


def weight_grads(x, s, d_act, hidden):
    g_first = jnp.einsum("sd,sf->df", x, d_act, preferred_element_type=jnp.float32)
    g_second = jnp.einsum("sf,sd->fd", hidden, s, preferred_element_type=jnp.float32)
    return g_first, g_second


def columns_joined(low, high, half):
    x = jnp.concatenate([low[:, :half], high[:, :half]], axis=1)
    s = jnp.concatenate([low[:, half:], high[:, half:]], axis=1)
    return x, s


def local(moe_input, out_grad, gate, route, w_in, b_in, w_out, qkv):
    tok_rows, width = moe_input.shape
    experts = lax.axis_size("ex")
    capacity = max(2, 2 * tok_rows // experts)
    half = width // lax.axis_size("hh")
    member = lax.axis_index("hh")
    heads_here = HEADS // lax.axis_size("hh")
    lead = SHIFT * CELLS
    start = WIN_T * CELLS - lead
    choose = route[:, 0]
    onehot = (choose[:, None] == jnp.arange(experts, dtype=jnp.int32)[None, :]).astype(jnp.bfloat16)
    earlier = (jnp.arange(tok_rows)[:, None] > jnp.arange(tok_rows)[None, :]).astype(jnp.bfloat16)
    before = jnp.dot(earlier, onehot, preferred_element_type=jnp.float32)
    slots = jnp.sum(before * onehot.astype(jnp.float32), axis=1).astype(jnp.int32)
    dest = choose * capacity + slots
    place = (dest[None, :] == jnp.arange(experts * capacity, dtype=jnp.int32)[:, None]).astype(jnp.bfloat16)
    own_x = lax.dynamic_slice_in_dim(moe_input, member * half, half, 1)
    own_grad = lax.dynamic_slice_in_dim(out_grad, member * half, half, 1)
    own_s = (gate[:, None] * own_grad.astype(jnp.float32)).astype(jnp.bfloat16)
    tokens = jnp.concatenate([own_x, own_s], axis=1)
    send = jnp.dot(place, tokens, preferred_element_type=jnp.float32).astype(jnp.bfloat16)
    send = send.reshape(experts, capacity, 2 * half)
    if capacity % 16 == 0 and experts % 4 == 0 and experts & (experts - 1) == 0:
        got, d_act, hidden, g_bias, qkv_edge, cot_edge, d_heads = exchange(
            send, qkv, w_in[0], b_in, w_out[0], place.T, own_grad, lead
        )
        g_bias = g_bias[0]
        got = got.reshape(2, experts * capacity, 2 * half)
        got_x, got_s = columns_joined(got[0], got[1], half)
        g_first, g_second = weight_grads(got_x, got_s, d_act, hidden)
    else:
        qkv_edge = passed_along(qkv[:, start:], "ex", 1)
        got = lax.all_to_all(send, "ex", split_axis=0, concat_axis=0, tiled=True)
        got = got.reshape(experts * capacity, 2 * half)
        other = passed_along(got, "hh", 1)
        first, second = jnp.where(member == 0, got, other), jnp.where(member == 0, other, got)
        got_x, got_s = columns_joined(first, second, half)
        d_inputs, g_first, g_bias, g_second = expert_terms(got_x, got_s, w_in[0], b_in[0], w_out[0])
        kept = lax.dynamic_slice_in_dim(d_inputs, member * half, half, 1)
        given = lax.dynamic_slice_in_dim(d_inputs, (1 - member) * half, half, 1).astype(jnp.bfloat16)
        d_rows = (kept + passed_along(given, "hh", 1).astype(jnp.float32)).astype(jnp.bfloat16)
        returned = lax.all_to_all(
            d_rows.reshape(experts, capacity, half), "ex", split_axis=0, concat_axis=0, tiled=True
        ).reshape(experts * capacity, half)
        d_moe = lax.dot_general(place, returned, (((0,), (0,)), ((), ())), preferred_element_type=jnp.float32)
        d_heads = (own_grad.astype(jnp.float32) + d_moe).astype(jnp.bfloat16)
        cot_edge = passed_along(d_heads[start:], "ex", 1)
    bias = jnp.where(lax.axis_index("ex") == 0, -1e30, 0.0).astype(jnp.float32).reshape(1)
    back, mine = window_grads(bias, qkv_edge, qkv, cot_edge, d_heads, heads_here)
    g_qkv = jnp.concatenate([mine, passed_along(back, "ex", -1)], axis=1)
    return (g_first[None], g_bias[None], g_second[None], g_qkv)


def solution(mesh):
    in_specs = (
        P("ex", None),
        P("ex", None),
        P("ex"),
        P("ex", None),
        P("ex", None, "hh"),
        P("ex", "hh"),
        P("ex", "hh", None),
        P(None, "ex", "hh"),
    )
    out_specs = (P("ex", None, "hh"), P("ex", "hh"), P("ex", "hh", None), P(None, "ex", "hh"))
    return jax.shard_map(local, mesh=mesh, in_specs=in_specs, out_specs=out_specs, check_vma=False)
```

```python
import functools
import math

import jax
import jax.numpy as jnp
from jax import lax
from jax.experimental import pallas as pl
from jax.experimental.pallas import tpu as pltpu
from jax.sharding import PartitionSpec as P

HEADS = 16
CELLS = 64
WIN_T = 8
SHIFT = 4


def passed_along(block, axis, distance):
    devices = range(lax.axis_size(axis))
    route = [((i - distance) % len(devices), i) for i in devices]
    return lax.ppermute(block, axis, route)


def gelu_parts(act):
    cdf = 0.5 * (1.0 + lax.erf(act * 0.7071067811865476))
    dens = jnp.exp(-0.5 * act * act) * 0.3989422804014327
    return (act * cdf, cdf + act * dens)


def expert_terms(inputs, scaled, w_first, bias, w_second):
    act = jnp.dot(inputs, w_first, preferred_element_type=jnp.float32) + bias
    value, slope = gelu_parts(act)
    hidden = value.astype(jnp.bfloat16)
    d_hidden = jnp.einsum("sd,fd->sf", scaled, w_second, preferred_element_type=jnp.float32)
    d_pre = d_hidden * slope
    d_act = d_pre.astype(jnp.bfloat16)
    d_inputs = jnp.einsum("sf,df->sd", d_act, w_first, preferred_element_type=jnp.float32)
    g_first = jnp.einsum("sd,sf->df", inputs, d_act, preferred_element_type=jnp.float32)
    g_bias = jnp.sum(d_pre, axis=0)
    g_second = jnp.einsum("sf,sd->fd", hidden, scaled, preferred_element_type=jnp.float32)
    return (d_inputs, g_first, g_bias, g_second)


def window_probs(heads, lead, bias, keys, q_t, probs_ref):
    cols, rows = q_t.shape
    head_dim = cols // heads
    factor = head_dim ** (-0.5) * math.log2(math.e)
    column = lax.broadcasted_iota(jnp.int32, (1, cols), 1)
    for head in range(heads):
        own = (column // head_dim == head).astype(jnp.float32).astype(jnp.bfloat16)
        keys_h = keys * own
        for part in range(2):
            span = slice(0, lead) if part == 0 else slice(lead, rows)
            scores = jnp.dot(keys_h, q_t[:, span], preferred_element_type=jnp.float32)
            low, high = scores[:lead], scores[lead:]
            if part == 0:
                high = high + bias
            else:
                low = low + bias
            scores = jnp.concatenate([low, high], axis=0)
            peak = jnp.max(scores, axis=0, keepdims=True)
            expo = jnp.exp2((scores - peak) * factor)
            probs = expo * (1.0 / jnp.sum(expo, axis=0, keepdims=True))
            probs_ref[head, :, span] = probs.astype(jnp.bfloat16)


def probs_kernel(heads, bias_ref, edge_ref, own_ref, probs_ref, q_t):
    lead, rows = edge_ref.shape[1], q_t.shape[1]
    queries = jnp.concatenate([edge_ref[0], own_ref[0, : rows - lead]], axis=0)
    keys = jnp.concatenate([edge_ref[1], own_ref[1, : rows - lead]], axis=0)
    q_t[...] = queries.T
    window_probs(heads, lead, bias_ref[0], keys, q_t, probs_ref)


def separate_probs(bias, edge, own, heads):
    _, rows, cols = own.shape
    vmem = pl.BlockSpec(memory_space=pltpu.VMEM)
    return pl.pallas_call(
        functools.partial(probs_kernel, heads),
        out_shape=jax.ShapeDtypeStruct((heads, rows, rows), jnp.bfloat16),
        in_specs=[pl.BlockSpec(memory_space=pltpu.SMEM), vmem, vmem],
        out_specs=vmem,
        scratch_shapes=[pltpu.VMEM((cols, rows), jnp.bfloat16)],
        compiler_params=pltpu.CompilerParams(vmem_limit_bytes=48 * 1024 * 1024),
        name="window_probs",
    )(bias, edge, own)


def window_kernel(heads, probs_ref, edge_ref, own_ref, cot_edge_ref, cot_ref, back_ref, mine_ref,
                  k_t, cot_t, dq_t):
    lead = edge_ref.shape[1]
    rows, cols = k_t.shape[1], k_t.shape[0]
    head_dim = cols // heads
    scale = head_dim ** (-0.5)
    queries = jnp.concatenate([edge_ref[0], own_ref[0, : rows - lead]], axis=0)
    keys = jnp.concatenate([edge_ref[1], own_ref[1, : rows - lead]], axis=0)
    values = jnp.concatenate([edge_ref[2], own_ref[2, : rows - lead]], axis=0)
    cot = jnp.concatenate([cot_edge_ref[...], cot_ref[: rows - lead]], axis=0)
    k_t[...] = keys.T
    cot_t[...] = cot.T
    column = lax.broadcasted_iota(jnp.int32, (1, cols), 1)
    d_k = d_v = None
    for head in range(heads):
        own = (column // head_dim == head).astype(jnp.float32).astype(jnp.bfloat16)
        values_h, queries_h, cot_h = values * own, queries * own, cot * own
        for part in range(2):
            span = slice(0, lead) if part == 0 else slice(lead, rows)
            probs_b = probs_ref[head, :, span]
            probs = probs_b.astype(jnp.float32)
            d_probs = jnp.dot(values_h, cot_t[:, span], preferred_element_type=jnp.float32)
            delta = jnp.sum(probs * d_probs, axis=0, keepdims=True)
            d_scores = (probs * (d_probs - delta)).astype(jnp.bfloat16)
            mine = slice(head * head_dim, (head + 1) * head_dim)
            dq_t[mine, span] = jnp.dot(k_t[mine, :], d_scores, preferred_element_type=jnp.float32) * scale
            more_k = jnp.dot(d_scores, queries_h[span], preferred_element_type=jnp.float32)
            more_v = jnp.dot(probs_b, cot_h[span], preferred_element_type=jnp.float32)
            d_k = more_k if d_k is None else d_k + more_k
            d_v = more_v if d_v is None else d_v + more_v
    d_q = dq_t[...].T.astype(jnp.bfloat16)
    for place, grad in enumerate((d_q, (d_k * scale).astype(jnp.bfloat16), d_v.astype(jnp.bfloat16))):
        back_ref[place] = grad[:lead]
        mine_ref[place] = grad[lead:]


def window_grads(probs, edge, own, cot_edge, cot, part, parts):
    lead = edge.shape[1]
    rows, cols = cot.shape
    heads, cols = probs.shape[0] // parts, cols // parts
    vmem = pl.BlockSpec(memory_space=pltpu.VMEM)
    return pl.pallas_call(
        functools.partial(window_kernel, heads),
        grid=(1,),
        out_shape=(
            jax.ShapeDtypeStruct((3, lead, cols), jnp.bfloat16),
            jax.ShapeDtypeStruct((3, rows - lead, cols), jnp.bfloat16),
        ),
        in_specs=[
            pl.BlockSpec((heads, rows, rows), lambda i: (part, 0, 0)),
            pl.BlockSpec((3, lead, cols), lambda i: (0, 0, part)),
            pl.BlockSpec((3, rows, cols), lambda i: (0, 0, part)),
            pl.BlockSpec((lead, cols), lambda i: (0, part)),
            pl.BlockSpec((rows, cols), lambda i: (0, part)),
        ],
        out_specs=(vmem, vmem),
        scratch_shapes=[
            pltpu.VMEM((cols, rows), jnp.bfloat16),
            pltpu.VMEM((cols, rows), jnp.bfloat16),
            pltpu.VMEM((cols, rows), jnp.float32),
        ],
        compiler_params=pltpu.CompilerParams(vmem_limit_bytes=48 * 1024 * 1024),
        cost_estimate=pl.CostEstimate(
            flops=8 * rows * rows * cols * heads, bytes_accessed=14 * rows * cols, transcendentals=0
        ),
        name="window_grads",
    )(probs, edge, own, cot_edge, cot)


MESH = pl.DeviceIdType.MESH


def exchange_kernel(n, group, heads, qkv_hbm, w_in_hbm, w_out_hbm, x_ref, grad_ref, gate_ref, route_ref, b_ref,
                    got_ref, dact_ref, hidden_ref, gb_ref, edge_ref, cot_edge_ref, heads_ref, probs_ref,
                    send_ref, place_t_ref, qkv_ref, w_in_ref, w_out_ref, q_t,
                    w_in_t, w_out_t, part_out, part_in, ret_out, ret_in,
                    send_sem, recv_sem, on_send, on_recv, part_send, part_recv, ret_send, ret_recv,
                    edge_sem, cot_sem, own_sem, load_sem):
    loads = [
        pltpu.make_async_copy(src, dst, load_sem.at[i])
        for i, (src, dst) in enumerate(((qkv_hbm, qkv_ref), (w_in_hbm, w_in_ref), (w_out_hbm, w_out_ref)))
    ]
    for load in loads:
        load.start()
    me, core = lax.axis_index("ex"), lax.axis_index("hh")
    after, sibling = lax.rem(me + 1, n), 1 - core
    capacity, half = ret_in.shape[1], ret_in.shape[2]
    rows = group * capacity
    lead = edge_ref.shape[1]
    start = qkv_ref.shape[1] - lead
    hidden_units = w_in_ref.shape[1]
    bits = n.bit_length() - 1

    def partner(k):
        total = 0
        for b in range(bits):
            bit = lax.rem(lax.div(me, 1 << b), 2)
            total = total + ((1 - bit) if (k >> b) & 1 else bit) * (1 << b)
        return total

    partners = [partner(k) for k in range(n)]
    barrier = pltpu.get_barrier_semaphore()
    for k in range(1, n):
        pl.semaphore_signal(barrier, inc=1, device_id=(partners[k], core), device_id_type=MESH)
    pl.semaphore_signal(barrier, inc=1, device_id=(me, sibling), device_id_type=MESH)
    pl.semaphore_wait(barrier, n)
    edge = pltpu.make_async_remote_copy(
        src_ref=qkv_hbm.at[:, pl.ds(start, lead)], dst_ref=edge_ref, send_sem=edge_sem.at[0],
        recv_sem=edge_sem.at[1], device_id=(after, core), device_id_type=MESH,
    )
    edge.start()

    tokens, width = x_ref.shape
    route = route_ref[...].astype(jnp.float32)
    expert = lax.broadcasted_iota(jnp.int32, (1, 128), 1).astype(jnp.float32)
    onehot = (route == expert).astype(jnp.float32)
    earlier = (
        lax.broadcasted_iota(jnp.int32, (tokens, tokens), 0) > lax.broadcasted_iota(jnp.int32, (tokens, tokens), 1)
    ).astype(jnp.float32).astype(jnp.bfloat16)
    before = jnp.dot(earlier, onehot.astype(jnp.bfloat16), preferred_element_type=jnp.float32)
    dest = route * float(capacity) + jnp.sum(before * onehot, axis=1, keepdims=True)
    slot = lax.broadcasted_iota(jnp.int32, (1, n * capacity), 1).astype(jnp.float32)
    place_t = (dest == slot).astype(jnp.float32).astype(jnp.bfloat16)
    place_t_ref[...] = place_t
    own_x = jnp.where(core == 0, x_ref[:, :half], x_ref[:, half:])
    own_grad = jnp.where(core == 0, grad_ref[:, :half], grad_ref[:, half:]).astype(jnp.float32)
    own_s = (gate_ref[...] * own_grad).astype(jnp.bfloat16)
    ready = jnp.dot(place_t.T, jnp.concatenate([own_x, own_s], axis=1), preferred_element_type=jnp.float32)
    send_ref[...] = ready.astype(jnp.bfloat16).reshape(n, capacity, 2 * half)

    def remote(src, dst, send, recv, device):
        return pltpu.make_async_remote_copy(
            src_ref=src, dst_ref=dst, send_sem=send, recv_sem=recv, device_id=device, device_id_type=MESH
        )

    out = {
        k: remote(send_ref.at[partners[k]], got_ref.at[core, me], send_sem.at[k], recv_sem.at[k],
                  (partners[k], core))
        for k in range(1, n)
    }
    passed = {
        k: remote(got_ref.at[core, partners[k]], got_ref.at[core, partners[k]], on_send.at[k], on_recv.at[k],
                  (me, sibling))
        for k in range(n)
    }
    far = list(range(n // 2, n))
    near = list(range(1, n // 2))
    order = []
    while far or near:
        order += near[:1] + far[:1]
        far, near = far[1:], near[1:]
    for k in order:
        out[k].start()
    own = pltpu.make_async_copy(send_ref.at[me], got_ref.at[core, me], own_sem.at[0])
    own.start()
    for load in loads:
        load.wait()
    w_in_t[...] = w_in_ref[...].T
    w_out_t[...] = w_out_ref[...].T

    back = {}
    parts = []
    step = hidden_units // 4
    bias_sums = [0.0] * 4
    for g in range(n // group):
        ks = range(g * group, (g + 1) * group)
        for k in ks:
            if k == 0:
                own.wait()
            else:
                out[k].wait_recv()
            passed[k].start()
        for k in ks:
            passed[k].wait_recv()
        base = lax.div(partners[g * group], group) * group
        low = got_ref[0, pl.ds(base, group)].reshape(rows, 2 * half)
        high = got_ref[1, pl.ds(base, group)].reshape(rows, 2 * half)
        x = jnp.concatenate([low[:, :half], high[:, :half]], axis=1)
        s = jnp.concatenate([low[:, half:], high[:, half:]], axis=1)
        span = pl.ds(pl.multiple_of(base * capacity, rows), rows)
        d_rows = None
        for c in range(4):
            cols = slice(c * step, (c + 1) * step)
            act = jnp.dot(x, w_in_ref[:, cols], preferred_element_type=jnp.float32) + b_ref[:, cols]
            value, slope = gelu_parts(act)
            hidden_ref[span, cols] = value.astype(jnp.bfloat16)
            d_pre = jnp.dot(s, w_out_t[:, cols], preferred_element_type=jnp.float32) * slope
            d_act = d_pre.astype(jnp.bfloat16)
            dact_ref[span, cols] = d_act
            bias_sums[c] = bias_sums[c] + jnp.sum(d_pre, axis=0, keepdims=True)
            more = jnp.dot(d_act, w_in_t[cols, :], preferred_element_type=jnp.float32)
            d_rows = more if d_rows is None else d_rows + more
        kept = jnp.where(core == 0, d_rows[:, :half], d_rows[:, half:])
        given = jnp.where(core == 0, d_rows[:, half:], d_rows[:, :half])
        part_out[g] = given.astype(jnp.bfloat16)
        swap = remote(part_out.at[g], part_in.at[g], part_send.at[g], part_recv.at[g], (me, sibling))
        swap.start()
        parts.append(swap)
        swap.wait_recv()
        total = (kept + part_in[g].astype(jnp.float32)).astype(jnp.bfloat16)
        ret_out[pl.ds(base, group)] = total.reshape(group, capacity, half)
        for k in reversed(ks):
            if k == 0:
                back[k] = pltpu.make_async_copy(ret_out.at[me], ret_in.at[me], own_sem.at[1])
            else:
                back[k] = remote(ret_out.at[partners[k]], ret_in.at[me], ret_send.at[k], ret_recv.at[k],
                                 (partners[k], core))
            back[k].start()
        if g == 1:
            edge.wait_recv()
            window = qkv_ref.shape[1]
            queries = jnp.concatenate([edge_ref[0], qkv_ref[0, : window - lead]], axis=0)
            keys = jnp.concatenate([edge_ref[1], qkv_ref[1, : window - lead]], axis=0)
            q_t[...] = queries.T
            bias = jnp.where(me == 0, -1e30, 0.0).astype(jnp.float32)
            window_probs(heads, lead, bias, keys, q_t, probs_ref)
    for c in range(4):
        gb_ref[:, c * step : (c + 1) * step] = bias_sums[c]

    total = jnp.where(core == 0, grad_ref[:, :half], grad_ref[:, half:]).astype(jnp.float32)
    for g in range(n // group):
        for k in range(g * group, (g + 1) * group):
            if k == 0:
                back[k].wait()
            else:
                back[k].wait_recv()
        base = lax.div(partners[g * group], group) * group
        span = pl.ds(pl.multiple_of(base * capacity, rows), rows)
        total = total + jnp.dot(
            place_t_ref[:, span], ret_in[pl.ds(base, group)].reshape(rows, half),
            preferred_element_type=jnp.float32,
        )
    heads_ref[...] = total.astype(jnp.bfloat16)
    cot = remote(heads_ref.at[pl.ds(start, lead)], cot_edge_ref, cot_sem.at[0], cot_sem.at[1], (after, core))
    cot.start()
    for k in range(n):
        passed[k].wait_send()
        if k > 0:
            out[k].wait_send()
            back[k].wait_send()
    for swap in parts:
        swap.wait_send()
    edge.wait_send()
    cot.wait()


def exchange(qkv, w_in, w_out, x, grad, gate, route, b_in, n, capacity, lead, heads):
    tokens, width = x.shape
    hidden_units = w_in.shape[1]
    half = qkv.shape[2]
    columns = 2 * half
    group = 4
    vmem = pl.BlockSpec(memory_space=pltpu.VMEM)
    bf16, f32 = jnp.bfloat16, jnp.float32
    dma = pltpu.SemaphoreType.DMA
    shape = jax.ShapeDtypeStruct
    return pl.pallas_call(
        functools.partial(exchange_kernel, n, group, heads),
        out_shape=(
            shape((2, n, capacity, columns), bf16),
            shape((n * capacity, hidden_units), bf16),
            shape((n * capacity, hidden_units), bf16),
            shape((1, hidden_units), f32),
            shape((3, lead, half), bf16),
            shape((lead, half), bf16),
            shape((tokens, half), bf16),
            shape((heads, tokens, tokens), bf16),
        ),
        in_specs=[pl.BlockSpec(memory_space=pl.ANY)] * 3 + [vmem] * 5,
        out_specs=[vmem] * 8,
        scratch_shapes=[
            pltpu.VMEM((n, capacity, columns), bf16),
            pltpu.VMEM((tokens, n * capacity), bf16),
            pltpu.VMEM(qkv.shape, bf16),
            pltpu.VMEM(w_in.shape, bf16),
            pltpu.VMEM(w_out.shape, bf16),
            pltpu.VMEM((half, tokens), bf16),
            pltpu.VMEM((hidden_units, width), bf16),
            pltpu.VMEM((width, hidden_units), bf16),
            pltpu.VMEM((n // group, group * capacity, half), bf16),
            pltpu.VMEM((n // group, group * capacity, half), bf16),
            pltpu.VMEM((n, capacity, half), bf16),
            pltpu.VMEM((n, capacity, half), bf16),
            dma((n,)), dma((n,)), dma((n,)), dma((n,)),
            dma((n // group,)), dma((n // group,)),
            dma((n,)), dma((n,)),
            dma((2,)), dma((2,)), dma((2,)), dma((3,)),
        ],
        compiler_params=pltpu.CompilerParams(
            collective_id=0, has_side_effects=True, vmem_limit_bytes=48 * 1024 * 1024
        ),
        cost_estimate=pl.CostEstimate(
            flops=6 * n * capacity * width * hidden_units, bytes_accessed=16 * 1024 * 1024,
            transcendentals=2 * n * capacity * hidden_units,
        ),
        name="exchange",
    )(qkv, w_in, w_out, x, grad, gate, route, b_in)


def weight_grads(x, s, d_act, hidden):
    g_first = jnp.einsum("sd,sf->df", x, d_act, preferred_element_type=jnp.float32)
    g_second = jnp.einsum("sf,sd->fd", hidden, s, preferred_element_type=jnp.float32)
    return g_first, g_second


def columns_joined(low, high, half):
    x = jnp.concatenate([low[:, :half], high[:, :half]], axis=1)
    s = jnp.concatenate([low[:, half:], high[:, half:]], axis=1)
    return x, s


def local(moe_input, out_grad, gate, route, w_in, b_in, w_out, qkv):
    tok_rows, width = moe_input.shape
    experts = lax.axis_size("ex")
    capacity = max(2, 2 * tok_rows // experts)
    half = width // lax.axis_size("hh")
    member = lax.axis_index("hh")
    heads_here = HEADS // lax.axis_size("hh")
    lead = SHIFT * CELLS
    start = WIN_T * CELLS - lead
    if capacity % 16 == 0 and experts % 4 == 0 and experts & (experts - 1) == 0:
        got, d_act, hidden, g_bias, qkv_edge, cot_edge, d_heads, probs = exchange(
            qkv, w_in[0], w_out[0], moe_input, out_grad, gate[:, None], route, b_in, experts, capacity, lead, heads_here
        )
        g_bias = g_bias[0]
        got = got.reshape(2, experts * capacity, 2 * half)
        got_x, got_s = columns_joined(got[0], got[1], half)
        g_first, g_second = weight_grads(got_x, got_s, d_act, hidden)
    else:
        choose = route[:, 0]
        onehot = (choose[:, None] == jnp.arange(experts, dtype=jnp.int32)[None, :]).astype(jnp.bfloat16)
        earlier = (jnp.arange(tok_rows)[:, None] > jnp.arange(tok_rows)[None, :]).astype(jnp.bfloat16)
        before = jnp.dot(earlier, onehot, preferred_element_type=jnp.float32)
        slots = jnp.sum(before * onehot.astype(jnp.float32), axis=1).astype(jnp.int32)
        dest = choose * capacity + slots
        place = (dest[None, :] == jnp.arange(experts * capacity, dtype=jnp.int32)[:, None]).astype(jnp.bfloat16)
        own_x = lax.dynamic_slice_in_dim(moe_input, member * half, half, 1)
        own_grad = lax.dynamic_slice_in_dim(out_grad, member * half, half, 1)
        own_s = (gate[:, None] * own_grad.astype(jnp.float32)).astype(jnp.bfloat16)
        tokens = jnp.concatenate([own_x, own_s], axis=1)
        send = jnp.dot(place, tokens, preferred_element_type=jnp.float32).astype(jnp.bfloat16)
        send = send.reshape(experts, capacity, 2 * half)
        qkv_edge = passed_along(qkv[:, start:], "ex", 1)
        got = lax.all_to_all(send, "ex", split_axis=0, concat_axis=0, tiled=True)
        got = got.reshape(experts * capacity, 2 * half)
        other = passed_along(got, "hh", 1)
        first, second = jnp.where(member == 0, got, other), jnp.where(member == 0, other, got)
        got_x, got_s = columns_joined(first, second, half)
        d_inputs, g_first, g_bias, g_second = expert_terms(got_x, got_s, w_in[0], b_in[0], w_out[0])
        kept = lax.dynamic_slice_in_dim(d_inputs, member * half, half, 1)
        given = lax.dynamic_slice_in_dim(d_inputs, (1 - member) * half, half, 1).astype(jnp.bfloat16)
        d_rows = (kept + passed_along(given, "hh", 1).astype(jnp.float32)).astype(jnp.bfloat16)
        returned = lax.all_to_all(
            d_rows.reshape(experts, capacity, half), "ex", split_axis=0, concat_axis=0, tiled=True
        ).reshape(experts * capacity, half)
        d_moe = lax.dot_general(place, returned, (((0,), (0,)), ((), ())), preferred_element_type=jnp.float32)
        d_heads = (own_grad.astype(jnp.float32) + d_moe).astype(jnp.bfloat16)
        cot_edge = passed_along(d_heads[start:], "ex", 1)
        bias = jnp.where(lax.axis_index("ex") == 0, -1e30, 0.0).astype(jnp.float32).reshape(1)
        probs = separate_probs(bias, qkv_edge, qkv, heads_here)
    pieces = []
    for part in range(2):
        back, mine = window_grads(probs, qkv_edge, qkv, cot_edge, d_heads, part, 2)
        pieces.append(jnp.concatenate([mine, passed_along(back, "ex", -1)], axis=1))
    g_qkv = jnp.concatenate(pieces, axis=2)
    return (g_first[None], g_bias[None], g_second[None], g_qkv)


def solution(mesh):
    in_specs = (
        P("ex", None),
        P("ex", None),
        P("ex"),
        P("ex", None),
        P("ex", None, "hh"),
        P("ex", "hh"),
        P("ex", "hh", None),
        P(None, "ex", "hh"),
    )
    out_specs = (P("ex", None, "hh"), P("ex", "hh"), P("ex", "hh", None), P(None, "ex", "hh"))
    return jax.shard_map(local, mesh=mesh, in_specs=in_specs, out_specs=out_specs, check_vma=False)
```

```python
import functools
import math

import jax
import jax.numpy as jnp
from jax import lax
from jax.experimental import pallas as pl
from jax.experimental.pallas import tpu as pltpu
from jax.sharding import PartitionSpec as P

HEADS = 16
CELLS = 64
WIN_T = 8
SHIFT = 4


def passed_along(block, axis, distance):
    devices = range(lax.axis_size(axis))
    route = [((i - distance) % len(devices), i) for i in devices]
    return lax.ppermute(block, axis, route)


def gelu_parts(act):
    cdf = 0.5 * (1.0 + lax.erf(act * 0.7071067811865476))
    dens = jnp.exp(-0.5 * act * act) * 0.3989422804014327
    return (act * cdf, cdf + act * dens)


def expert_terms(inputs, scaled, w_first, bias, w_second):
    act = jnp.dot(inputs, w_first, preferred_element_type=jnp.float32) + bias
    value, slope = gelu_parts(act)
    hidden = value.astype(jnp.bfloat16)
    d_hidden = jnp.einsum("sd,fd->sf", scaled, w_second, preferred_element_type=jnp.float32)
    d_pre = d_hidden * slope
    d_act = d_pre.astype(jnp.bfloat16)
    d_inputs = jnp.einsum("sf,df->sd", d_act, w_first, preferred_element_type=jnp.float32)
    g_first = jnp.einsum("sd,sf->df", inputs, d_act, preferred_element_type=jnp.float32)
    g_bias = jnp.sum(d_pre, axis=0)
    g_second = jnp.einsum("sf,sd->fd", hidden, scaled, preferred_element_type=jnp.float32)
    return (d_inputs, g_first, g_bias, g_second)


def window_kernel(heads, bias_ref, edge_ref, own_ref, cot_edge_ref, cot_ref, back_ref, mine_ref,
                  q_t, k_t, cot_t, dq_t):
    lead = edge_ref.shape[1]
    rows, cols = k_t.shape[1], k_t.shape[0]
    head_dim = cols // heads
    scale = head_dim ** (-0.5)
    factor = scale * math.log2(math.e)
    queries = jnp.concatenate([edge_ref[0], own_ref[0, : rows - lead]], axis=0)
    keys = jnp.concatenate([edge_ref[1], own_ref[1, : rows - lead]], axis=0)
    values = jnp.concatenate([edge_ref[2], own_ref[2, : rows - lead]], axis=0)
    cot = jnp.concatenate([cot_edge_ref[...], cot_ref[: rows - lead]], axis=0)
    q_t[...] = queries.T
    k_t[...] = keys.T
    cot_t[...] = cot.T
    column = lax.broadcasted_iota(jnp.int32, (1, cols), 1)
    d_k = d_v = None
    for head in range(heads):
        own = (column // head_dim == head).astype(jnp.float32).astype(jnp.bfloat16)
        keys_h, values_h, queries_h, cot_h = keys * own, values * own, queries * own, cot * own
        for part in range(2):
            span = slice(0, lead) if part == 0 else slice(lead, rows)
            scores = jnp.dot(keys_h, q_t[:, span], preferred_element_type=jnp.float32)
            low, high = scores[:lead], scores[lead:]
            if part == 0:
                high = high + bias_ref[0]
            else:
                low = low + bias_ref[0]
            scores = jnp.concatenate([low, high], axis=0)
            peak = jnp.max(scores, axis=0, keepdims=True)
            expo = jnp.exp2((scores - peak) * factor)
            probs = expo * (1.0 / jnp.sum(expo, axis=0, keepdims=True))
            probs_b = probs.astype(jnp.bfloat16)
            d_probs = jnp.dot(values_h, cot_t[:, span], preferred_element_type=jnp.float32)
            delta = jnp.sum(probs * d_probs, axis=0, keepdims=True)
            d_scores = (probs * (d_probs - delta)).astype(jnp.bfloat16)
            mine = slice(head * head_dim, (head + 1) * head_dim)
            dq_t[mine, span] = jnp.dot(k_t[mine, :], d_scores, preferred_element_type=jnp.float32) * scale
            more_k = jnp.dot(d_scores, queries_h[span], preferred_element_type=jnp.float32)
            more_v = jnp.dot(probs_b, cot_h[span], preferred_element_type=jnp.float32)
            d_k = more_k if d_k is None else d_k + more_k
            d_v = more_v if d_v is None else d_v + more_v
    d_q = dq_t[...].T.astype(jnp.bfloat16)
    for place, grad in enumerate((d_q, (d_k * scale).astype(jnp.bfloat16), d_v.astype(jnp.bfloat16))):
        back_ref[place] = grad[:lead]
        mine_ref[place] = grad[lead:]


def window_grads(bias, edge, own, cot_edge, cot, heads, part, parts):
    lead = edge.shape[1]
    rows, cols = cot.shape
    heads, cols = heads // parts, cols // parts
    vmem = pl.BlockSpec(memory_space=pltpu.VMEM)
    return pl.pallas_call(
        functools.partial(window_kernel, heads),
        grid=(1,),
        out_shape=(
            jax.ShapeDtypeStruct((3, lead, cols), jnp.bfloat16),
            jax.ShapeDtypeStruct((3, rows - lead, cols), jnp.bfloat16),
        ),
        in_specs=[
            pl.BlockSpec(memory_space=pltpu.SMEM),
            pl.BlockSpec((3, lead, cols), lambda i: (0, 0, part)),
            pl.BlockSpec((3, rows, cols), lambda i: (0, 0, part)),
            pl.BlockSpec((lead, cols), lambda i: (0, part)),
            pl.BlockSpec((rows, cols), lambda i: (0, part)),
        ],
        out_specs=(vmem, vmem),
        scratch_shapes=[
            pltpu.VMEM((cols, rows), jnp.bfloat16),
            pltpu.VMEM((cols, rows), jnp.bfloat16),
            pltpu.VMEM((cols, rows), jnp.bfloat16),
            pltpu.VMEM((cols, rows), jnp.float32),
        ],
        compiler_params=pltpu.CompilerParams(vmem_limit_bytes=48 * 1024 * 1024),
        cost_estimate=pl.CostEstimate(
            flops=10 * rows * rows * cols * heads, bytes_accessed=14 * rows * cols,
            transcendentals=heads * rows * rows,
        ),
        name="window_grads",
    )(bias, edge, own, cot_edge, cot)


MESH = pl.DeviceIdType.MESH


def exchange_kernel(n, group, qkv_hbm, w_in_hbm, w_out_hbm, x_ref, grad_ref, gate_ref, route_ref, b_ref,
                    got_out, dact_out, hidden_out, gb_ref, edge_ref, cot_edge_ref, heads_ref,
                    got_ref, dact_ref, hidden_ref, send_ref, place_t_ref, w_in_ref, w_out_ref,
                    w_in_t, w_out_t, part_out, part_in, ret_out, ret_in,
                    send_sem, recv_sem, on_send, on_recv, part_send, part_recv, ret_send, ret_recv,
                    edge_sem, cot_sem, own_sem, load_sem, keep_sem):
    loads = [
        pltpu.make_async_copy(src, dst, load_sem.at[i])
        for i, (src, dst) in enumerate(((w_in_hbm, w_in_ref), (w_out_hbm, w_out_ref)))
    ]
    for load in loads:
        load.start()
    me, core = lax.axis_index("ex"), lax.axis_index("hh")
    after, sibling = lax.rem(me + 1, n), 1 - core
    capacity, half = ret_in.shape[1], ret_in.shape[2]
    rows = group * capacity
    lead = edge_ref.shape[1]
    start = qkv_hbm.shape[1] - lead
    hidden_units = w_in_ref.shape[1]
    bits = n.bit_length() - 1

    def partner(k):
        total = 0
        for b in range(bits):
            bit = lax.rem(lax.div(me, 1 << b), 2)
            total = total + ((1 - bit) if (k >> b) & 1 else bit) * (1 << b)
        return total

    partners = [partner(k) for k in range(n)]
    barrier = pltpu.get_barrier_semaphore()
    for k in range(1, n):
        pl.semaphore_signal(barrier, inc=1, device_id=(partners[k], core), device_id_type=MESH)
    pl.semaphore_signal(barrier, inc=1, device_id=(me, sibling), device_id_type=MESH)
    pl.semaphore_wait(barrier, n)
    edge = pltpu.make_async_remote_copy(
        src_ref=qkv_hbm.at[:, pl.ds(start, lead)], dst_ref=edge_ref, send_sem=edge_sem.at[0],
        recv_sem=edge_sem.at[1], device_id=(after, core), device_id_type=MESH,
    )
    edge.start()

    tokens, width = x_ref.shape
    route = route_ref[...].astype(jnp.float32)
    expert = lax.broadcasted_iota(jnp.int32, (1, 128), 1).astype(jnp.float32)
    onehot = (route == expert).astype(jnp.float32)
    earlier = (
        lax.broadcasted_iota(jnp.int32, (tokens, tokens), 0) > lax.broadcasted_iota(jnp.int32, (tokens, tokens), 1)
    ).astype(jnp.float32).astype(jnp.bfloat16)
    before = jnp.dot(earlier, onehot.astype(jnp.bfloat16), preferred_element_type=jnp.float32)
    dest = route * float(capacity) + jnp.sum(before * onehot, axis=1, keepdims=True)
    slot = lax.broadcasted_iota(jnp.int32, (1, n * capacity), 1).astype(jnp.float32)
    place_t = (dest == slot).astype(jnp.float32).astype(jnp.bfloat16)
    place_t_ref[...] = place_t
    own_x = jnp.where(core == 0, x_ref[:, :half], x_ref[:, half:])
    own_grad = jnp.where(core == 0, grad_ref[:, :half], grad_ref[:, half:]).astype(jnp.float32)
    own_s = (gate_ref[...] * own_grad).astype(jnp.bfloat16)
    ready = jnp.dot(place_t.T, jnp.concatenate([own_x, own_s], axis=1), preferred_element_type=jnp.float32)
    send_ref[...] = ready.astype(jnp.bfloat16).reshape(n, capacity, 2 * half)

    def remote(src, dst, send, recv, device):
        return pltpu.make_async_remote_copy(
            src_ref=src, dst_ref=dst, send_sem=send, recv_sem=recv, device_id=device, device_id_type=MESH
        )

    out = {
        k: remote(send_ref.at[partners[k]], got_ref.at[core, me], send_sem.at[k], recv_sem.at[k],
                  (partners[k], core))
        for k in range(1, n)
    }
    passed = {
        k: remote(got_ref.at[core, partners[k]], got_ref.at[core, partners[k]], on_send.at[k], on_recv.at[k],
                  (me, sibling))
        for k in range(n)
    }
    far = list(range(n // 2, n))
    near = list(range(1, n // 2))
    order = []
    while far or near:
        order += near[:1] + far[:1]
        far, near = far[1:], near[1:]
    for k in order:
        out[k].start()
    own = pltpu.make_async_copy(send_ref.at[me], got_ref.at[core, me], own_sem.at[0])
    own.start()
    for load in loads:
        load.wait()
    w_in_t[...] = w_in_ref[...].T
    w_out_t[...] = w_out_ref[...].T

    back = {}
    parts = []
    kept_out = []
    step = hidden_units // 4
    bias_sums = [0.0] * 4
    for g in range(n // group):
        ks = range(g * group, (g + 1) * group)
        for k in ks:
            if k == 0:
                own.wait()
            else:
                out[k].wait_recv()
            passed[k].start()
        for k in ks:
            passed[k].wait_recv()
        base = lax.div(partners[g * group], group) * group
        low = got_ref[0, pl.ds(base, group)].reshape(rows, 2 * half)
        high = got_ref[1, pl.ds(base, group)].reshape(rows, 2 * half)
        x = jnp.concatenate([low[:, :half], high[:, :half]], axis=1)
        s = jnp.concatenate([low[:, half:], high[:, half:]], axis=1)
        span = pl.ds(pl.multiple_of(base * capacity, rows), rows)
        d_rows = None
        for c in range(4):
            cols = slice(c * step, (c + 1) * step)
            act = jnp.dot(x, w_in_ref[:, cols], preferred_element_type=jnp.float32) + b_ref[:, cols]
            value, slope = gelu_parts(act)
            hidden_ref[span, cols] = value.astype(jnp.bfloat16)
            d_pre = jnp.dot(s, w_out_t[:, cols], preferred_element_type=jnp.float32) * slope
            d_act = d_pre.astype(jnp.bfloat16)
            dact_ref[span, cols] = d_act
            bias_sums[c] = bias_sums[c] + jnp.sum(d_pre, axis=0, keepdims=True)
            more = jnp.dot(d_act, w_in_t[cols, :], preferred_element_type=jnp.float32)
            d_rows = more if d_rows is None else d_rows + more
        kept = jnp.where(core == 0, d_rows[:, :half], d_rows[:, half:])
        given = jnp.where(core == 0, d_rows[:, half:], d_rows[:, :half])
        part_out[g] = given.astype(jnp.bfloat16)
        swap = remote(part_out.at[g], part_in.at[g], part_send.at[g], part_recv.at[g], (me, sibling))
        swap.start()
        parts.append(swap)
        swap.wait_recv()
        total = (kept + part_in[g].astype(jnp.float32)).astype(jnp.bfloat16)
        ret_out[pl.ds(base, group)] = total.reshape(group, capacity, half)
        for k in reversed(ks):
            if k == 0:
                back[k] = pltpu.make_async_copy(ret_out.at[me], ret_in.at[me], own_sem.at[1])
            else:
                back[k] = remote(ret_out.at[partners[k]], ret_in.at[me], ret_send.at[k], ret_recv.at[k],
                                 (partners[k], core))
            back[k].start()
        for i, (src, dst) in enumerate(
            ((got_ref.at[:, pl.ds(base, group)], got_out.at[:, pl.ds(base, group)]),
             (dact_ref.at[span], dact_out.at[span]), (hidden_ref.at[span], hidden_out.at[span]))
        ):
            keep = pltpu.make_async_copy(src, dst, keep_sem.at[g, i])
            keep.start()
            kept_out.append(keep)
    for c in range(4):
        gb_ref[:, c * step : (c + 1) * step] = bias_sums[c]

    total = jnp.where(core == 0, grad_ref[:, :half], grad_ref[:, half:]).astype(jnp.float32)
    for g in range(n // group):
        for k in range(g * group, (g + 1) * group):
            if k == 0:
                back[k].wait()
            else:
                back[k].wait_recv()
        base = lax.div(partners[g * group], group) * group
        span = pl.ds(pl.multiple_of(base * capacity, rows), rows)
        total = total + jnp.dot(
            place_t_ref[:, span], ret_in[pl.ds(base, group)].reshape(rows, half),
            preferred_element_type=jnp.float32,
        )
    heads_ref[...] = total.astype(jnp.bfloat16)
    cot = remote(heads_ref.at[pl.ds(start, lead)], cot_edge_ref, cot_sem.at[0], cot_sem.at[1], (after, core))
    cot.start()
    for k in range(n):
        passed[k].wait_send()
        if k > 0:
            out[k].wait_send()
            back[k].wait_send()
    for swap in parts:
        swap.wait_send()
    for keep in kept_out:
        keep.wait()
    edge.wait()
    cot.wait()


def exchange(qkv, w_in, w_out, x, grad, gate, route, b_in, n, capacity, lead):
    tokens, width = x.shape
    hidden_units = w_in.shape[1]
    half = qkv.shape[2]
    columns = 2 * half
    group = 4
    vmem = pl.BlockSpec(memory_space=pltpu.VMEM)
    bf16, f32 = jnp.bfloat16, jnp.float32
    dma = pltpu.SemaphoreType.DMA
    shape = jax.ShapeDtypeStruct
    return pl.pallas_call(
        functools.partial(exchange_kernel, n, group),
        out_shape=(
            shape((2, n, capacity, columns), bf16),
            shape((n * capacity, hidden_units), bf16),
            shape((n * capacity, hidden_units), bf16),
            shape((1, hidden_units), f32),
            shape((3, lead, half), bf16),
            shape((lead, half), bf16),
            shape((tokens, half), bf16),
        ),
        in_specs=[pl.BlockSpec(memory_space=pl.ANY)] * 3 + [vmem] * 5,
        out_specs=[pl.BlockSpec(memory_space=pl.ANY)] * 3 + [vmem] * 4,
        scratch_shapes=[
            pltpu.VMEM((2, n, capacity, columns), bf16),
            pltpu.VMEM((n * capacity, hidden_units), bf16),
            pltpu.VMEM((n * capacity, hidden_units), bf16),
            pltpu.VMEM((n, capacity, columns), bf16),
            pltpu.VMEM((tokens, n * capacity), bf16),
            pltpu.VMEM(w_in.shape, bf16),
            pltpu.VMEM(w_out.shape, bf16),
            pltpu.VMEM((hidden_units, width), bf16),
            pltpu.VMEM((width, hidden_units), bf16),
            pltpu.VMEM((n // group, group * capacity, half), bf16),
            pltpu.VMEM((n // group, group * capacity, half), bf16),
            pltpu.VMEM((n, capacity, half), bf16),
            pltpu.VMEM((n, capacity, half), bf16),
            dma((n,)), dma((n,)), dma((n,)), dma((n,)),
            dma((n // group,)), dma((n // group,)),
            dma((n,)), dma((n,)),
            dma((2,)), dma((2,)), dma((2,)), dma((2,)), dma((n // group, 3)),
        ],
        compiler_params=pltpu.CompilerParams(
            collective_id=0, has_side_effects=True, vmem_limit_bytes=60 * 1024 * 1024
        ),
        cost_estimate=pl.CostEstimate(
            flops=6 * n * capacity * width * hidden_units, bytes_accessed=16 * 1024 * 1024,
            transcendentals=2 * n * capacity * hidden_units,
        ),
        name="exchange",
    )(qkv, w_in, w_out, x, grad, gate, route, b_in)


def weight_grads(x, s, d_act, hidden):
    g_first = jnp.einsum("sd,sf->df", x, d_act, preferred_element_type=jnp.float32)
    g_second = jnp.einsum("sf,sd->fd", hidden, s, preferred_element_type=jnp.float32)
    return g_first, g_second


def columns_joined(low, high, half):
    x = jnp.concatenate([low[:, :half], high[:, :half]], axis=1)
    s = jnp.concatenate([low[:, half:], high[:, half:]], axis=1)
    return x, s


def local(moe_input, out_grad, gate, route, w_in, b_in, w_out, qkv):
    tok_rows, width = moe_input.shape
    experts = lax.axis_size("ex")
    capacity = max(2, 2 * tok_rows // experts)
    half = width // lax.axis_size("hh")
    member = lax.axis_index("hh")
    heads_here = HEADS // lax.axis_size("hh")
    lead = SHIFT * CELLS
    start = WIN_T * CELLS - lead
    if capacity % 16 == 0 and experts % 4 == 0 and experts & (experts - 1) == 0:
        got, d_act, hidden, g_bias, qkv_edge, cot_edge, d_heads = exchange(
            qkv, w_in[0], w_out[0], moe_input, out_grad, gate[:, None], route, b_in, experts, capacity, lead
        )
        g_bias = g_bias[0]
        got = got.reshape(2, experts * capacity, 2 * half)
        got_x, got_s = columns_joined(got[0], got[1], half)
        g_first, g_second = weight_grads(got_x, got_s, d_act, hidden)
    else:
        choose = route[:, 0]
        onehot = (choose[:, None] == jnp.arange(experts, dtype=jnp.int32)[None, :]).astype(jnp.bfloat16)
        earlier = (jnp.arange(tok_rows)[:, None] > jnp.arange(tok_rows)[None, :]).astype(jnp.bfloat16)
        before = jnp.dot(earlier, onehot, preferred_element_type=jnp.float32)
        slots = jnp.sum(before * onehot.astype(jnp.float32), axis=1).astype(jnp.int32)
        dest = choose * capacity + slots
        place = (dest[None, :] == jnp.arange(experts * capacity, dtype=jnp.int32)[:, None]).astype(jnp.bfloat16)
        own_x = lax.dynamic_slice_in_dim(moe_input, member * half, half, 1)
        own_grad = lax.dynamic_slice_in_dim(out_grad, member * half, half, 1)
        own_s = (gate[:, None] * own_grad.astype(jnp.float32)).astype(jnp.bfloat16)
        tokens = jnp.concatenate([own_x, own_s], axis=1)
        send = jnp.dot(place, tokens, preferred_element_type=jnp.float32).astype(jnp.bfloat16)
        send = send.reshape(experts, capacity, 2 * half)
        qkv_edge = passed_along(qkv[:, start:], "ex", 1)
        got = lax.all_to_all(send, "ex", split_axis=0, concat_axis=0, tiled=True)
        got = got.reshape(experts * capacity, 2 * half)
        other = passed_along(got, "hh", 1)
        first, second = jnp.where(member == 0, got, other), jnp.where(member == 0, other, got)
        got_x, got_s = columns_joined(first, second, half)
        d_inputs, g_first, g_bias, g_second = expert_terms(got_x, got_s, w_in[0], b_in[0], w_out[0])
        kept = lax.dynamic_slice_in_dim(d_inputs, member * half, half, 1)
        given = lax.dynamic_slice_in_dim(d_inputs, (1 - member) * half, half, 1).astype(jnp.bfloat16)
        d_rows = (kept + passed_along(given, "hh", 1).astype(jnp.float32)).astype(jnp.bfloat16)
        returned = lax.all_to_all(
            d_rows.reshape(experts, capacity, half), "ex", split_axis=0, concat_axis=0, tiled=True
        ).reshape(experts * capacity, half)
        d_moe = lax.dot_general(place, returned, (((0,), (0,)), ((), ())), preferred_element_type=jnp.float32)
        d_heads = (own_grad.astype(jnp.float32) + d_moe).astype(jnp.bfloat16)
        cot_edge = passed_along(d_heads[start:], "ex", 1)
    bias = jnp.where(lax.axis_index("ex") == 0, -1e30, 0.0).astype(jnp.float32).reshape(1)
    pieces = []
    for part in range(2):
        back, mine = window_grads(bias, qkv_edge, qkv, cot_edge, d_heads, heads_here, part, 2)
        pieces.append(jnp.concatenate([mine, passed_along(back, "ex", -1)], axis=1))
    g_qkv = jnp.concatenate(pieces, axis=2)
    return (g_first[None], g_bias[None], g_second[None], g_qkv)


def solution(mesh):
    in_specs = (
        P("ex", None),
        P("ex", None),
        P("ex"),
        P("ex", None),
        P("ex", None, "hh"),
        P("ex", "hh"),
        P("ex", "hh", None),
        P(None, "ex", "hh"),
    )
    out_specs = (P("ex", None, "hh"), P("ex", "hh"), P("ex", "hh", None), P(None, "ex", "hh"))
    return jax.shard_map(local, mesh=mesh, in_specs=in_specs, out_specs=out_specs, check_vma=False)
```

```python
import functools
import math

import jax
import jax.numpy as jnp
from jax import lax
from jax.experimental import pallas as pl
from jax.experimental.pallas import tpu as pltpu
from jax.sharding import PartitionSpec as P

HEADS = 16
CELLS = 64
WIN_T = 8
SHIFT = 4


def passed_along(block, axis, distance):
    devices = range(lax.axis_size(axis))
    route = [((i - distance) % len(devices), i) for i in devices]
    return lax.ppermute(block, axis, route)


def gelu_parts(act):
    cdf = 0.5 * (1.0 + lax.erf(act * 0.7071067811865476))
    dens = jnp.exp(-0.5 * act * act) * 0.3989422804014327
    return (act * cdf, cdf + act * dens)


def expert_terms(inputs, scaled, w_first, bias, w_second):
    act = jnp.dot(inputs, w_first, preferred_element_type=jnp.float32) + bias
    value, slope = gelu_parts(act)
    hidden = value.astype(jnp.bfloat16)
    d_hidden = jnp.einsum("sd,fd->sf", scaled, w_second, preferred_element_type=jnp.float32)
    d_pre = d_hidden * slope
    d_act = d_pre.astype(jnp.bfloat16)
    d_inputs = jnp.einsum("sf,df->sd", d_act, w_first, preferred_element_type=jnp.float32)
    g_first = jnp.einsum("sd,sf->df", inputs, d_act, preferred_element_type=jnp.float32)
    g_bias = jnp.sum(d_pre, axis=0)
    g_second = jnp.einsum("sf,sd->fd", hidden, scaled, preferred_element_type=jnp.float32)
    return (d_inputs, g_first, g_bias, g_second)


def window_kernel(heads, bias_ref, edge_ref, own_ref, cot_edge_ref, cot_ref, back_ref, mine_ref,
                  q_t, k_t, cot_t, dq_t):
    lead = edge_ref.shape[1]
    rows, cols = k_t.shape[1], k_t.shape[0]
    head_dim = cols // heads
    scale = head_dim ** (-0.5)
    factor = scale * math.log2(math.e)
    queries = jnp.concatenate([edge_ref[0], own_ref[0, : rows - lead]], axis=0)
    keys = jnp.concatenate([edge_ref[1], own_ref[1, : rows - lead]], axis=0)
    values = jnp.concatenate([edge_ref[2], own_ref[2, : rows - lead]], axis=0)
    cot = jnp.concatenate([cot_edge_ref[...], cot_ref[: rows - lead]], axis=0)
    q_t[...] = queries.T
    k_t[...] = keys.T
    cot_t[...] = cot.T
    column = lax.broadcasted_iota(jnp.int32, (1, cols), 1)
    d_k = d_v = None
    for head in range(heads):
        own = (column // head_dim == head).astype(jnp.float32).astype(jnp.bfloat16)
        keys_h, values_h, queries_h, cot_h = keys * own, values * own, queries * own, cot * own
        for part in range(2):
            span = slice(0, lead) if part == 0 else slice(lead, rows)
            scores = jnp.dot(keys_h, q_t[:, span], preferred_element_type=jnp.float32)
            low, high = scores[:lead], scores[lead:]
            if part == 0:
                high = high + bias_ref[0]
            else:
                low = low + bias_ref[0]
            scores = jnp.concatenate([low, high], axis=0)
            peak = jnp.max(scores, axis=0, keepdims=True)
            expo = jnp.exp2((scores - peak) * factor)
            probs = expo * (1.0 / jnp.sum(expo, axis=0, keepdims=True))
            probs_b = probs.astype(jnp.bfloat16)
            d_probs = jnp.dot(values_h, cot_t[:, span], preferred_element_type=jnp.float32)
            delta = jnp.sum(probs * d_probs, axis=0, keepdims=True)
            d_scores = (probs * (d_probs - delta)).astype(jnp.bfloat16)
            mine = slice(head * head_dim, (head + 1) * head_dim)
            dq_t[mine, span] = jnp.dot(k_t[mine, :], d_scores, preferred_element_type=jnp.float32) * scale
            more_k = jnp.dot(d_scores, queries_h[span], preferred_element_type=jnp.float32)
            more_v = jnp.dot(probs_b, cot_h[span], preferred_element_type=jnp.float32)
            d_k = more_k if d_k is None else d_k + more_k
            d_v = more_v if d_v is None else d_v + more_v
    d_q = dq_t[...].T.astype(jnp.bfloat16)
    for place, grad in enumerate((d_q, (d_k * scale).astype(jnp.bfloat16), d_v.astype(jnp.bfloat16))):
        back_ref[place] = grad[:lead]
        mine_ref[place] = grad[lead:]


def window_grads(bias, edge, own, cot_edge, cot, heads, part, parts):
    lead = edge.shape[1]
    rows, cols = cot.shape
    heads, cols = heads // parts, cols // parts
    vmem = pl.BlockSpec(memory_space=pltpu.VMEM)
    return pl.pallas_call(
        functools.partial(window_kernel, heads),
        grid=(1,),
        out_shape=(
            jax.ShapeDtypeStruct((3, lead, cols), jnp.bfloat16),
            jax.ShapeDtypeStruct((3, rows - lead, cols), jnp.bfloat16),
        ),
        in_specs=[
            pl.BlockSpec(memory_space=pltpu.SMEM),
            pl.BlockSpec((3, lead, cols), lambda i: (0, 0, part)),
            pl.BlockSpec((3, rows, cols), lambda i: (0, 0, part)),
            pl.BlockSpec((lead, cols), lambda i: (0, part)),
            pl.BlockSpec((rows, cols), lambda i: (0, part)),
        ],
        out_specs=(vmem, vmem),
        scratch_shapes=[
            pltpu.VMEM((cols, rows), jnp.bfloat16),
            pltpu.VMEM((cols, rows), jnp.bfloat16),
            pltpu.VMEM((cols, rows), jnp.bfloat16),
            pltpu.VMEM((cols, rows), jnp.float32),
        ],
        compiler_params=pltpu.CompilerParams(vmem_limit_bytes=60 * 1024 * 1024),
        cost_estimate=pl.CostEstimate(
            flops=10 * rows * rows * cols * heads, bytes_accessed=14 * rows * cols,
            transcendentals=heads * rows * rows,
        ),
        name="window_grads",
    )(bias, edge, own, cot_edge, cot)


MESH = pl.DeviceIdType.MESH


def exchange_kernel(n, groups, qkv_hbm, w_in_hbm, w_out_hbm, x_ref, grad_ref, gate_ref, route_ref, b_ref,
                    got_out, dact_out, hidden_out, gb_ref, edge_ref, cot_edge_ref, heads_ref,
                    got_ref, dact_ref, hidden_ref, send_ref, place_t_ref, w_in_ref, w_out_ref,
                    w_in_t, w_out_t, part_out, part_in, ret_out, ret_in,
                    send_sem, recv_sem, on_send, on_recv, part_send, part_recv, ret_send, ret_recv,
                    edge_sem, cot_sem, own_sem, load_sem, keep_sem):
    loads = [
        pltpu.make_async_copy(src, dst, load_sem.at[i])
        for i, (src, dst) in enumerate(((w_in_hbm, w_in_ref), (w_out_hbm, w_out_ref)))
    ]
    for load in loads:
        load.start()
    me, core = lax.axis_index("ex"), lax.axis_index("hh")
    after, sibling = lax.rem(me + 1, n), 1 - core
    capacity, half = ret_in.shape[1], ret_in.shape[2]
    lead = edge_ref.shape[1]
    start = qkv_hbm.shape[1] - lead
    hidden_units = w_in_ref.shape[1]
    bits = n.bit_length() - 1

    def partner(k):
        total = 0
        for b in range(bits):
            bit = lax.rem(lax.div(me, 1 << b), 2)
            total = total + ((1 - bit) if (k >> b) & 1 else bit) * (1 << b)
        return total

    partners = [partner(k) for k in range(n)]
    barrier = pltpu.get_barrier_semaphore()
    for k in range(1, n):
        pl.semaphore_signal(barrier, inc=1, device_id=(partners[k], core), device_id_type=MESH)
    pl.semaphore_signal(barrier, inc=1, device_id=(me, sibling), device_id_type=MESH)
    pl.semaphore_wait(barrier, n)
    edge = pltpu.make_async_remote_copy(
        src_ref=qkv_hbm.at[:, pl.ds(start, lead)], dst_ref=edge_ref, send_sem=edge_sem.at[0],
        recv_sem=edge_sem.at[1], device_id=(after, core), device_id_type=MESH,
    )
    edge.start()

    tokens, width = x_ref.shape
    route = jnp.broadcast_to(route_ref[...].astype(jnp.float32), (8, tokens)).T[:, :1]
    gate = jnp.broadcast_to(gate_ref[...], (8, tokens)).T[:, :1]
    expert = lax.broadcasted_iota(jnp.int32, (1, 128), 1).astype(jnp.float32)
    onehot = (route == expert).astype(jnp.float32)
    earlier = (
        lax.broadcasted_iota(jnp.int32, (tokens, tokens), 0) > lax.broadcasted_iota(jnp.int32, (tokens, tokens), 1)
    ).astype(jnp.float32).astype(jnp.bfloat16)
    before = jnp.dot(earlier, onehot.astype(jnp.bfloat16), preferred_element_type=jnp.float32)
    dest = route * float(capacity) + jnp.sum(before * onehot, axis=1, keepdims=True)
    slot = lax.broadcasted_iota(jnp.int32, (1, n * capacity), 1).astype(jnp.float32)
    place_t = (dest == slot).astype(jnp.float32).astype(jnp.bfloat16)
    place_t_ref[...] = place_t
    own_x = jnp.where(core == 0, x_ref[:, :half], x_ref[:, half:])
    own_grad = jnp.where(core == 0, grad_ref[:, :half], grad_ref[:, half:]).astype(jnp.float32)
    own_s = (gate * own_grad).astype(jnp.bfloat16)
    ready = jnp.dot(place_t.T, jnp.concatenate([own_x, own_s], axis=1), preferred_element_type=jnp.float32)
    send_ref[...] = ready.astype(jnp.bfloat16).reshape(n, capacity, 2 * half)

    def remote(src, dst, send, recv, device):
        return pltpu.make_async_remote_copy(
            src_ref=src, dst_ref=dst, send_sem=send, recv_sem=recv, device_id=device, device_id_type=MESH
        )

    out = {
        k: remote(send_ref.at[partners[k]], got_ref.at[core, me], send_sem.at[k], recv_sem.at[k],
                  (partners[k], core))
        for k in range(1, n)
    }
    passed = {
        k: remote(got_ref.at[core, partners[k]], got_ref.at[core, partners[k]], on_send.at[k], on_recv.at[k],
                  (me, sibling))
        for k in range(n)
    }
    far = list(range(n // 2, n))
    near = list(range(1, n // 2))
    order = []
    while far or near:
        order += near[:1] + far[:1]
        far, near = far[1:], near[1:]
    for k in order:
        out[k].start()
    own = pltpu.make_async_copy(send_ref.at[me], got_ref.at[core, me], own_sem.at[0])
    own.start()
    for load in loads:
        load.wait()
    w_in_t[...] = w_in_ref[...].T
    w_out_t[...] = w_out_ref[...].T

    back = {}
    parts = []
    kept_out = []
    step = hidden_units // 4
    bias_sums = [0.0] * 4
    for g, ks in enumerate(groups):
        group, rows = len(ks), len(ks) * capacity
        for k in ks:
            if k == 0:
                own.wait()
            else:
                out[k].wait_recv()
            passed[k].start()
        for k in ks:
            passed[k].wait_recv()
        base = lax.div(partners[ks[0]], group) * group
        low = got_ref[0, pl.ds(base, group)].reshape(rows, 2 * half)
        high = got_ref[1, pl.ds(base, group)].reshape(rows, 2 * half)
        x = jnp.concatenate([low[:, :half], high[:, :half]], axis=1)
        s = jnp.concatenate([low[:, half:], high[:, half:]], axis=1)
        span = pl.ds(pl.multiple_of(base * capacity, rows), rows)
        d_rows = None
        for c in range(4):
            cols = slice(c * step, (c + 1) * step)
            act = jnp.dot(x, w_in_ref[:, cols], preferred_element_type=jnp.float32) + b_ref[:, cols]
            value, slope = gelu_parts(act)
            hidden_ref[span, cols] = value.astype(jnp.bfloat16)
            d_pre = jnp.dot(s, w_out_t[:, cols], preferred_element_type=jnp.float32) * slope
            d_act = d_pre.astype(jnp.bfloat16)
            dact_ref[span, cols] = d_act
            bias_sums[c] = bias_sums[c] + jnp.sum(d_pre, axis=0, keepdims=True)
            more = jnp.dot(d_act, w_in_t[cols, :], preferred_element_type=jnp.float32)
            d_rows = more if d_rows is None else d_rows + more
        kept = jnp.where(core == 0, d_rows[:, :half], d_rows[:, half:])
        given = jnp.where(core == 0, d_rows[:, half:], d_rows[:, :half])
        part_out[g, :rows] = given.astype(jnp.bfloat16)
        halves = pl.ds(0, rows)
        swap = remote(part_out.at[g, halves], part_in.at[g, halves], part_send.at[g], part_recv.at[g], (me, sibling))
        swap.start()
        parts.append(swap)
        swap.wait_recv()
        total = (kept + part_in[g, :rows].astype(jnp.float32)).astype(jnp.bfloat16)
        ret_out[pl.ds(base, group)] = total.reshape(group, capacity, half)
        for k in reversed(ks):
            if k == 0:
                back[k] = pltpu.make_async_copy(ret_out.at[me], ret_in.at[me], own_sem.at[1])
            else:
                back[k] = remote(ret_out.at[partners[k]], ret_in.at[me], ret_send.at[k], ret_recv.at[k],
                                 (partners[k], core))
            back[k].start()
        for i, (src, dst) in enumerate(
            ((got_ref.at[:, pl.ds(base, group)], got_out.at[:, pl.ds(base, group)]),
             (dact_ref.at[span], dact_out.at[span]), (hidden_ref.at[span], hidden_out.at[span]))
        ):
            keep = pltpu.make_async_copy(src, dst, keep_sem.at[g, i])
            keep.start()
            kept_out.append(keep)
    for c in range(4):
        gb_ref[:, c * step : (c + 1) * step] = bias_sums[c]

    total = jnp.where(core == 0, grad_ref[:, :half], grad_ref[:, half:]).astype(jnp.float32)
    for ks in groups:
        group, rows = len(ks), len(ks) * capacity
        for k in ks:
            if k == 0:
                back[k].wait()
            else:
                back[k].wait_recv()
        base = lax.div(partners[ks[0]], group) * group
        span = pl.ds(pl.multiple_of(base * capacity, rows), rows)
        total = total + jnp.dot(
            place_t_ref[:, span], ret_in[pl.ds(base, group)].reshape(rows, half),
            preferred_element_type=jnp.float32,
        )
    heads_ref[...] = total.astype(jnp.bfloat16)
    cot = remote(heads_ref.at[pl.ds(start, lead)], cot_edge_ref, cot_sem.at[0], cot_sem.at[1], (after, core))
    cot.start()
    for k in range(n):
        passed[k].wait_send()
        if k > 0:
            out[k].wait_send()
            back[k].wait_send()
    for swap in parts:
        swap.wait_send()
    for keep in kept_out:
        keep.wait()
    edge.wait()
    cot.wait()


def exchange(qkv, w_in, w_out, x, grad, gate, route, b_in, n, capacity, lead):
    tokens, width = x.shape
    hidden_units = w_in.shape[1]
    half = qkv.shape[2]
    columns = 2 * half
    groups = [range(k, k + 4) for k in range(0, n // 2, 4)] + [range(k, k + 2) for k in range(n // 2, n, 2)]
    count = len(groups)
    vmem = pl.BlockSpec(memory_space=pltpu.VMEM)
    bf16, f32 = jnp.bfloat16, jnp.float32
    dma = pltpu.SemaphoreType.DMA
    shape = jax.ShapeDtypeStruct
    return pl.pallas_call(
        functools.partial(exchange_kernel, n, groups),
        out_shape=(
            shape((2, n, capacity, columns), bf16),
            shape((n * capacity, hidden_units), bf16),
            shape((n * capacity, hidden_units), bf16),
            shape((1, hidden_units), f32),
            shape((3, lead, half), bf16),
            shape((lead, half), bf16),
            shape((tokens, half), bf16),
        ),
        in_specs=[pl.BlockSpec(memory_space=pl.ANY)] * 3 + [vmem] * 5,
        out_specs=[pl.BlockSpec(memory_space=pl.ANY)] * 3 + [vmem] * 4,
        scratch_shapes=[
            pltpu.VMEM((2, n, capacity, columns), bf16),
            pltpu.VMEM((n * capacity, hidden_units), bf16),
            pltpu.VMEM((n * capacity, hidden_units), bf16),
            pltpu.VMEM((n, capacity, columns), bf16),
            pltpu.VMEM((tokens, n * capacity), bf16),
            pltpu.VMEM(w_in.shape, bf16),
            pltpu.VMEM(w_out.shape, bf16),
            pltpu.VMEM((hidden_units, width), bf16),
            pltpu.VMEM((width, hidden_units), bf16),
            pltpu.VMEM((count, 4 * capacity, half), bf16),
            pltpu.VMEM((count, 4 * capacity, half), bf16),
            pltpu.VMEM((n, capacity, half), bf16),
            pltpu.VMEM((n, capacity, half), bf16),
            dma((n,)), dma((n,)), dma((n,)), dma((n,)),
            dma((count,)), dma((count,)),
            dma((n,)), dma((n,)),
            dma((2,)), dma((2,)), dma((2,)), dma((2,)), dma((count, 3)),
        ],
        compiler_params=pltpu.CompilerParams(
            collective_id=0, has_side_effects=True, vmem_limit_bytes=60 * 1024 * 1024
        ),
        cost_estimate=pl.CostEstimate(
            flops=6 * n * capacity * width * hidden_units, bytes_accessed=16 * 1024 * 1024,
            transcendentals=2 * n * capacity * hidden_units,
        ),
        name="exchange",
    )(qkv, w_in, w_out, x, grad, gate, route, b_in)


def weight_grads(x, s, d_act, hidden):
    g_first = jnp.einsum("sd,sf->df", x, d_act, preferred_element_type=jnp.float32)
    g_second = jnp.einsum("sf,sd->fd", hidden, s, preferred_element_type=jnp.float32)
    return g_first, g_second


def columns_joined(low, high, half):
    x = jnp.concatenate([low[:, :half], high[:, :half]], axis=1)
    s = jnp.concatenate([low[:, half:], high[:, half:]], axis=1)
    return x, s


def local(moe_input, out_grad, gate, route, w_in, b_in, w_out, qkv):
    tok_rows, width = moe_input.shape
    experts = lax.axis_size("ex")
    capacity = max(2, 2 * tok_rows // experts)
    half = width // lax.axis_size("hh")
    member = lax.axis_index("hh")
    heads_here = HEADS // lax.axis_size("hh")
    lead = SHIFT * CELLS
    start = WIN_T * CELLS - lead
    if capacity % 16 == 0 and experts % 8 == 0 and experts & (experts - 1) == 0:
        got, d_act, hidden, g_bias, qkv_edge, cot_edge, d_heads = exchange(
            qkv, w_in[0], w_out[0], moe_input, out_grad, gate[None], route.reshape(1, tok_rows), b_in, experts, capacity, lead
        )
        g_bias = g_bias[0]
        got = got.reshape(2, experts * capacity, 2 * half)
        got_x, got_s = columns_joined(got[0], got[1], half)
        g_first, g_second = weight_grads(got_x, got_s, d_act, hidden)
    else:
        choose = route[:, 0]
        onehot = (choose[:, None] == jnp.arange(experts, dtype=jnp.int32)[None, :]).astype(jnp.bfloat16)
        earlier = (jnp.arange(tok_rows)[:, None] > jnp.arange(tok_rows)[None, :]).astype(jnp.bfloat16)
        before = jnp.dot(earlier, onehot, preferred_element_type=jnp.float32)
        slots = jnp.sum(before * onehot.astype(jnp.float32), axis=1).astype(jnp.int32)
        dest = choose * capacity + slots
        place = (dest[None, :] == jnp.arange(experts * capacity, dtype=jnp.int32)[:, None]).astype(jnp.bfloat16)
        own_x = lax.dynamic_slice_in_dim(moe_input, member * half, half, 1)
        own_grad = lax.dynamic_slice_in_dim(out_grad, member * half, half, 1)
        own_s = (gate[:, None] * own_grad.astype(jnp.float32)).astype(jnp.bfloat16)
        tokens = jnp.concatenate([own_x, own_s], axis=1)
        send = jnp.dot(place, tokens, preferred_element_type=jnp.float32).astype(jnp.bfloat16)
        send = send.reshape(experts, capacity, 2 * half)
        qkv_edge = passed_along(qkv[:, start:], "ex", 1)
        got = lax.all_to_all(send, "ex", split_axis=0, concat_axis=0, tiled=True)
        got = got.reshape(experts * capacity, 2 * half)
        other = passed_along(got, "hh", 1)
        first, second = jnp.where(member == 0, got, other), jnp.where(member == 0, other, got)
        got_x, got_s = columns_joined(first, second, half)
        d_inputs, g_first, g_bias, g_second = expert_terms(got_x, got_s, w_in[0], b_in[0], w_out[0])
        kept = lax.dynamic_slice_in_dim(d_inputs, member * half, half, 1)
        given = lax.dynamic_slice_in_dim(d_inputs, (1 - member) * half, half, 1).astype(jnp.bfloat16)
        d_rows = (kept + passed_along(given, "hh", 1).astype(jnp.float32)).astype(jnp.bfloat16)
        returned = lax.all_to_all(
            d_rows.reshape(experts, capacity, half), "ex", split_axis=0, concat_axis=0, tiled=True
        ).reshape(experts * capacity, half)
        d_moe = lax.dot_general(place, returned, (((0,), (0,)), ((), ())), preferred_element_type=jnp.float32)
        d_heads = (own_grad.astype(jnp.float32) + d_moe).astype(jnp.bfloat16)
        cot_edge = passed_along(d_heads[start:], "ex", 1)
    bias = jnp.where(lax.axis_index("ex") == 0, -1e30, 0.0).astype(jnp.float32).reshape(1)
    pieces = []
    for part in range(2):
        back, mine = window_grads(bias, qkv_edge, qkv, cot_edge, d_heads, heads_here, part, 2)
        pieces.append(jnp.concatenate([mine, passed_along(back, "ex", -1)], axis=1))
    g_qkv = jnp.concatenate(pieces, axis=2)
    return (g_first[None], g_bias[None], g_second[None], g_qkv)


def solution(mesh):
    in_specs = (
        P("ex", None),
        P("ex", None),
        P("ex"),
        P("ex", None),
        P("ex", None, "hh"),
        P("ex", "hh"),
        P("ex", "hh", None),
        P(None, "ex", "hh"),
    )
    out_specs = (P("ex", None, "hh"), P("ex", "hh"), P("ex", "hh", None), P(None, "ex", "hh"))
    return jax.shard_map(local, mesh=mesh, in_specs=in_specs, out_specs=out_specs, check_vma=False)
```
